128 devices in a mesh: seq: 4 (over x_hi, core), res: 32 (over z, x_lo, y).
Axes of the slice: x: 4 (x_hi: 2, x_lo: 2; x = x_hi * 2 + x_lo), y: 4, z: 4, core: 2. Of those that a mesh axis runs over, the one named last changes fastest.
Arguments:
- normed_homolog_matrix: bfloat16 [4, 4096, 256], P('seq', 'res'), may hold values from -6 to 6
- result_cotangent: bfloat16 [4, 4096, 256], P('seq', 'res'), may hold values from -16 to 16
- question_matrix: bfloat16 [256, 256], replicated, may hold values from -0.375 to 0.375
- lookup_matrix: bfloat16 [256, 256], replicated, may hold values from -0.375 to 0.375
- content_matrix: bfloat16 [256, 256], replicated, may hold values from -0.375 to 0.375
- sigmoid_matrix: bfloat16 [256, 256], replicated, may hold values from -0.375 to 0.375
- result_matrix: bfloat16 [256, 256], replicated, may hold values from -0.375 to 0.375
- residue_pair_bias: bfloat16 [8, 4096, 4096], P(None, 'seq', 'res'), may hold values from -240 to 240
Outputs:
- homolog_derivative: bfloat16 [4, 4096, 256], P('seq', 'res')
- couple_offset_derivative: float32 [8, 4096, 4096], P(None, 'seq', 'res')
The draws below stay inside these ranges and needn't reach their ends.
All inputs are finite; a program needn't handle non-finite values.
Results may differ from the reference program's by a relative error of at most 0.028.
Values may be sent and summed in bfloat16 or wider, within the bound.
A program may use at most 192 MiB of HBM per device.

```python
import math
import jax
import jax.numpy as jnp
from jax import lax

HEAD_TOTAL = 8
HD = 32
FEATURE_DEPTH = 256
HOMOLOG_PORTION = 1
HOMOLOG_TOTAL = 4
CHAIN_LENGTH = 4096
N_SEQ = 4


def draw_residue_pair_bias(key, part):
    key_base, key_row, key_col = jax.random.split(key, 3)
    base_value = jnp.clip(jax.random.normal(key_base, (HEAD_TOTAL, CHAIN_LENGTH, CHAIN_LENGTH), jnp.float32), -4.0, 4.0)
    row_low = 0.3
    row_high = 3.0
    row_scale = jnp.exp(jax.random.uniform(key_row, (HEAD_TOTAL, CHAIN_LENGTH, 1), jnp.float32, math.log(row_low), math.log(row_high)))
    col_scale = jnp.exp(jax.random.uniform(key_col, (HEAD_TOTAL, 1, CHAIN_LENGTH), jnp.float32, math.log(0.55), math.log(1.8)))
    result = base_value * row_scale * col_scale
    return result.astype(jnp.bfloat16)


def levels(own_key, shape, cuts, least, largest):
    def one(dim, shards_of):
        heights = jax.random.uniform(jax.random.fold_in(jax.random.fold_in(own_key, 6), dim), (shards_of,), jnp.float32, least / len(cuts), largest / len(cuts))
        return jnp.repeat(jnp.exp(heights), shape[dim] // shards_of).reshape((-1,) + (1,) * (len(shape) - dim - 1))

    level = one(*cuts[0])
    for cut in cuts[1:]:
        level = level * one(*cut)
    return level


def noise(stream_key, extent, spread, bound, pieces=(), dtype=jnp.bfloat16):
    entries = jax.random.normal(stream_key, extent, jnp.float32) * spread
    if len(pieces) > 0:
        entries = levels(stream_key, extent, pieces, -0.22, 0.18) * entries
    return jnp.clip(entries, min=-bound, max=bound).astype(dtype)


def setup_inputs(seed: int = 0) -> dict:
    splits = jax.random.split(jax.random.key(seed), 9)
    normed_homolog_matrix = noise(splits[0], (HOMOLOG_TOTAL, CHAIN_LENGTH, FEATURE_DEPTH), 1.0, 6.0, ((0, 4), (1, 32)))
    result_cotangent = noise(splits[1], (HOMOLOG_TOTAL, CHAIN_LENGTH, FEATURE_DEPTH), 4.0, 16.0, ((0, 4), (1, 32)))
    question_matrix = noise(splits[2], (FEATURE_DEPTH, FEATURE_DEPTH), FEATURE_DEPTH ** -0.5, 0.375)
    lookup_matrix = noise(splits[3], (FEATURE_DEPTH, FEATURE_DEPTH), FEATURE_DEPTH ** -0.5, 0.375)
    content_matrix = noise(splits[4], (FEATURE_DEPTH, FEATURE_DEPTH), FEATURE_DEPTH ** -0.5, 0.375)
    sigmoid_matrix = noise(splits[5], (FEATURE_DEPTH, FEATURE_DEPTH), FEATURE_DEPTH ** -0.5, 0.375)
    result_matrix = noise(splits[6], (FEATURE_DEPTH, FEATURE_DEPTH), FEATURE_DEPTH ** -0.5, 0.375)
    residue_pair_bias = draw_residue_pair_bias(jax.random.fold_in(splits[8], 71), 0)
    return {"normed_homolog_matrix": normed_homolog_matrix, "result_cotangent": result_cotangent, "question_matrix": question_matrix, "lookup_matrix": lookup_matrix, "content_matrix": content_matrix, "sigmoid_matrix": sigmoid_matrix, "result_matrix": result_matrix, "residue_pair_bias": residue_pair_bias}


def lower_precision_convert(values):
    return lax.optimization_barrier(values.astype(jnp.bfloat16)).astype(jnp.float32)


def reference(normed_homolog_matrix, result_cotangent, question_matrix, lookup_matrix, content_matrix, sigmoid_matrix, result_matrix, residue_pair_bias):
    query_scaling = HD ** -0.5
    query_block = min(512, CHAIN_LENGTH)
    block_count = CHAIN_LENGTH // query_block
    finest_precision_mode = lax.Precision.HIGHEST
    row_starts = (jnp.arange(block_count) * query_block).astype(jnp.int32)

    def linear_map(flat_rows, weight):
        product = jnp.dot(flat_rows, weight, preferred_element_type=jnp.float32)
        return product.reshape(HOMOLOG_PORTION, CHAIN_LENGTH, HEAD_TOTAL, HD)

    def widened_matrix(weight):
        return weight.astype(jnp.float32).T

    def collect_row_slices(piled_matrix):
        return jnp.transpose(piled_matrix, (1, 0, 2, 3, 4)).reshape(HOMOLOG_PORTION * CHAIN_LENGTH, FEATURE_DEPTH)

    def each_block(bias_total, input_arrays):
        homolog_tile, tile_derivative = input_arrays
        homolog_matrix_reshaped = homolog_tile.reshape(HOMOLOG_PORTION * CHAIN_LENGTH, FEATURE_DEPTH)
        query_vectors = lower_precision_convert(linear_map(homolog_matrix_reshaped, question_matrix) * query_scaling)
        complete_keys = lower_precision_convert(linear_map(homolog_matrix_reshaped, lookup_matrix))
        complete_values = lower_precision_convert(linear_map(homolog_matrix_reshaped, content_matrix))
        gate_preactivation = linear_map(homolog_matrix_reshaped, sigmoid_matrix)
        sigmoid_derivative = linear_map(tile_derivative.reshape(HOMOLOG_PORTION * CHAIN_LENGTH, FEATURE_DEPTH), result_matrix.T)

        def per_rows(running, row_start):
            lookup_derivative, content_derivative = running
            query_rows = lax.dynamic_slice_in_dim(query_vectors, row_start, query_block, 1)
            bias_row_slices = lax.dynamic_slice_in_dim(residue_pair_bias, row_start, query_block, 1).astype(jnp.float32)
            scores = jnp.einsum("sihd,sjhd->shij", query_rows, complete_keys, precision=finest_precision_mode) + bias_row_slices[None]
            row_top = jnp.max(scores, -1, keepdims=True)
            log_total = row_top + jnp.log(jnp.sum(jnp.exp(scores - row_top), -1, keepdims=True))
            attn_probs = jnp.exp(scores - log_total)
            prob_low = lower_precision_convert(attn_probs)
            attn_out = jnp.einsum("shij,sjhd->sihd", prob_low, complete_values, precision=finest_precision_mode)
            gate_open = jax.nn.sigmoid(lax.dynamic_slice_in_dim(gate_preactivation, row_start, query_block, 1))
            grad_rows = lax.dynamic_slice_in_dim(sigmoid_derivative, row_start, query_block, 1)
            attn_grad = lower_precision_convert(grad_rows * gate_open)
            logit_grad = lower_precision_convert(grad_rows * attn_out * gate_open * (1.0 - gate_open))
            row_dot = jnp.transpose(jnp.sum(attn_grad * attn_out, -1), (0, 2, 1))[..., None]
            prob_grad = jnp.einsum("sihd,sjhd->shij", attn_grad, complete_values, precision=finest_precision_mode)
            score_grad = attn_probs * (prob_grad - row_dot)
            score_low = lower_precision_convert(score_grad)
            query_grad = lower_precision_convert(query_scaling * jnp.einsum("shij,sjhd->sihd", score_low, complete_keys, precision=finest_precision_mode))
            lookup_derivative = lookup_derivative + jnp.einsum("shij,sihd->sjhd", score_low, query_rows, precision=finest_precision_mode)
            content_derivative = content_derivative + jnp.einsum("shij,sihd->sjhd", prob_low, attn_grad, precision=finest_precision_mode)
            bias_part = lax.optimization_barrier(jnp.sum(score_grad, 0).astype(jnp.bfloat16))
            return (lookup_derivative, content_derivative), (query_grad, logit_grad, bias_part)

        zero_grad = jnp.zeros((HOMOLOG_PORTION, CHAIN_LENGTH, HEAD_TOTAL, HD), jnp.float32)
        running, piled_matrix = lax.scan(per_rows, (zero_grad, zero_grad), row_starts)
        lookup_derivative, content_derivative = running
        query_gradients, score_gradients, bias_parts = piled_matrix
        homolog_derivative = jnp.dot(collect_row_slices(query_gradients), widened_matrix(question_matrix), precision=finest_precision_mode)
        homolog_derivative = homolog_derivative + jnp.dot(collect_row_slices(score_gradients), widened_matrix(sigmoid_matrix), precision=finest_precision_mode)
        homolog_derivative = homolog_derivative + jnp.dot(lower_precision_convert(lookup_derivative).reshape(HOMOLOG_PORTION * CHAIN_LENGTH, FEATURE_DEPTH), widened_matrix(lookup_matrix), precision=finest_precision_mode)
        homolog_derivative = homolog_derivative + jnp.dot(lower_precision_convert(content_derivative).reshape(HOMOLOG_PORTION * CHAIN_LENGTH, FEATURE_DEPTH), widened_matrix(content_matrix), precision=finest_precision_mode)
        bias_full = jnp.transpose(bias_parts, (1, 0, 2, 3)).reshape(HEAD_TOTAL, CHAIN_LENGTH, CHAIN_LENGTH)
        renewed_accumulator = bias_total + bias_full.astype(jnp.float32)
        return renewed_accumulator, homolog_derivative.astype(jnp.bfloat16).reshape(HOMOLOG_PORTION, CHAIN_LENGTH, FEATURE_DEPTH)

    received_tiles = (normed_homolog_matrix.reshape(N_SEQ, HOMOLOG_PORTION, CHAIN_LENGTH, FEATURE_DEPTH), result_cotangent.reshape(N_SEQ, HOMOLOG_PORTION, CHAIN_LENGTH, FEATURE_DEPTH))
    couple_offset_derivative, homolog_tiles = lax.scan(each_block, jnp.zeros((HEAD_TOTAL, CHAIN_LENGTH, CHAIN_LENGTH), jnp.float32), received_tiles)
    return homolog_tiles.reshape(HOMOLOG_TOTAL, CHAIN_LENGTH, FEATURE_DEPTH), couple_offset_derivative
```

```python
import functools

import jax
import jax.numpy as jnp
from jax import lax
from jax.experimental import pallas as pl
from jax.experimental.pallas import tpu as pltpu
from jax.sharding import PartitionSpec as P

HEADS = 8
HD = 32
WIDTH = 256
ROWS = 1024
KEYS = 128
SEQS = 4
RES = 32
BLK = 128
CH = 256
F32 = jnp.float32
BF16 = jnp.bfloat16


def dot(a, b, dims):
    return lax.dot_general(a, b, (dims, ((), ())), preferred_element_type=F32)


NN = ((1,), (0,))
NT = ((1,), (1,))
TN = ((0,), (0,))


def load_chunk(qa_ref, s, which, h, c):
    rows = pl.ds(pl.multiple_of(h * HD, HD), HD)
    parts = [qa_ref[s * 8 + c * 2 + u, which, rows, :] for u in range(2)]
    return jnp.concatenate(parts, axis=1)


def stats_kernel(qa_ref, kh_ref, vh_ref, bias_ref, m_ref, l_ref, d_ref):
    def body(step, carry):
        h, c = step // 4, step % 4
        cols = pl.ds(pl.multiple_of(c * CH, CH), CH)
        bias = bias_ref[h, :, cols].astype(F32)
        for s in range(SEQS):
            qt = load_chunk(qa_ref, s, 0, h, c)
            at = load_chunk(qa_ref, s, 1, h, c)
            sc = dot(kh_ref[s, h], qt, NN) + bias
            top = jnp.max(sc, axis=0, keepdims=True)
            e = jnp.exp(sc - top)
            dp = dot(vh_ref[s, h], at, NN)
            m_ref[s, pl.ds(h, 1), cols] = top
            l_ref[s, pl.ds(h, 1), cols] = jnp.sum(e, axis=0, keepdims=True)
            d_ref[s, pl.ds(h, 1), cols] = jnp.sum(e * dp, axis=0, keepdims=True)
        return carry

    lax.fori_loop(0, 32, body, 0)


def grad_kernel(qa_ref, kh_ref, vh_ref, kt_ref, vt_ref, bias_ref, lt_ref, d_ref,
                od_ref, dk_ref, dv_ref, db_ref):
    dk_ref[...] = jnp.zeros_like(dk_ref)
    dv_ref[...] = jnp.zeros_like(dv_ref)

    def body(step, carry):
        h, c = step // 4, step % 4
        cols = pl.ds(pl.multiple_of(c * CH, CH), CH)
        rows = pl.ds(pl.multiple_of(h * HD, HD), HD)
        bias = bias_ref[h, :, cols].astype(F32)
        total = None
        for s in range(SEQS):
            qt = load_chunk(qa_ref, s, 0, h, c)
            at = load_chunk(qa_ref, s, 1, h, c)
            sc = dot(kh_ref[s, h], qt, NN) + bias
            p = jnp.exp(sc - lt_ref[s, pl.ds(h, 1), cols])
            dp = dot(vh_ref[s, h], at, NN)
            ds = p * (dp - d_ref[s, pl.ds(h, 1), cols])
            total = ds if total is None else total + ds
            pb = p.astype(BF16)
            db = ds.astype(BF16)
            o = dot(vt_ref[s, rows, :], pb, NN).astype(BF16)
            dq = dot(kt_ref[s, rows, :], db, NN).astype(BF16)
            for u in range(2):
                od_ref[s * 8 + c * 2 + u, 0, rows, :] = o[:, u * BLK:(u + 1) * BLK]
                od_ref[s * 8 + c * 2 + u, 1, rows, :] = dq[:, u * BLK:(u + 1) * BLK]
            dk_ref[s, h] += dot(db, qt, NT)
            dv_ref[s, h] += dot(pb, at, NT)
        for u in range(2):
            out = pl.ds(pl.multiple_of(c * CH + u * BLK, BLK), BLK)
            db_ref[h, out, :] = total[:, u * BLK:(u + 1) * BLK].T
        return carry

    lax.fori_loop(0, 32, body, 0)


def vmem(n):
    return [pl.BlockSpec(memory_space=pltpu.VMEM)] * n


def on_device(x, g, wq, wk, wv, wg, wr, bias):
    x, g = x[0], g[0]
    scale = HD ** -0.5
    qt = (dot(wq, x, ((0,), (1,))) * scale).astype(BF16)
    k = dot(x, wk, NN).astype(BF16)
    v = dot(x, wv, NN).astype(BF16)
    gate = jax.nn.sigmoid(dot(wg, x, ((0,), (1,))))
    gg = dot(wr, g, NT)
    at = (gg * gate).astype(BF16)
    swap = [(s * RES + z * 8 + t, z * RES + s * 8 + t) for s in range(4) for z in range(4) for t in range(8)]
    qa = lax.ppermute(jnp.stack([qt, at]), ("seq", "res"), swap)
    qa = lax.all_gather(qa, "res", axis=0, tiled=False)
    kv = lax.all_gather(jnp.stack([k, v]), "seq", axis=0, tiled=False)
    heads = kv.reshape(SEQS, 2, KEYS, HEADS, HD).transpose(1, 0, 3, 2, 4)
    flat = kv.transpose(1, 0, 3, 2)
    bias_t = bias.transpose(0, 2, 1)

    stat = jax.ShapeDtypeStruct((SEQS, HEADS, ROWS), F32)
    params = pltpu.CompilerParams(vmem_limit_bytes=48 * 2 ** 20)
    m, l, d = pl.pallas_call(
        stats_kernel, out_shape=[stat] * 3, in_specs=vmem(4), out_specs=vmem(3),
        compiler_params=params,
    )(qa, heads[0], heads[1], bias_t)
    top = lax.pmax(m, "res")
    fix = jnp.exp(m - top)
    both = lax.psum(jnp.stack([l * fix, d * fix]), "res")
    total = top + jnp.log(both[0])
    row_dot = both[1] / both[0]

    od, dk, dv, db = pl.pallas_call(
        grad_kernel,
        out_shape=[
            jax.ShapeDtypeStruct((RES, 2, WIDTH, BLK), BF16),
            jax.ShapeDtypeStruct((SEQS, HEADS, KEYS, HD), F32),
            jax.ShapeDtypeStruct((SEQS, HEADS, KEYS, HD), F32),
            jax.ShapeDtypeStruct((HEADS, ROWS, KEYS), F32),
        ],
        in_specs=vmem(8), out_specs=vmem(4),
        compiler_params=params,
    )(qa, heads[0], heads[1], flat[0], flat[1], bias_t, total, row_dot)

    od = lax.psum_scatter(od, "res", scatter_dimension=0, tiled=False)
    od = lax.ppermute(od, ("seq", "res"), swap)
    dkv = jnp.stack([dk, dv], axis=1).transpose(0, 1, 3, 2, 4).reshape(SEQS, 2, KEYS, WIDTH)
    dkv = lax.psum_scatter(dkv.astype(BF16), "seq", scatter_dimension=0, tiled=False)
    out = od[0].astype(F32)
    dq = (od[1].astype(F32) * scale).astype(BF16)
    dl = (gg * out * gate * (1.0 - gate)).astype(BF16)
    hom = dot(dq, wq, ((0,), (1,))) + dot(dl, wg, ((0,), (1,)))
    hom = hom + dot(dkv[0], wk, NT) + dot(dkv[1], wv, NT)
    return hom.astype(BF16)[None], db


def solution(mesh):
    return jax.shard_map(
        on_device,
        mesh=mesh,
        in_specs=(
            P("seq", "res", None), P("seq", "res", None), P(), P(), P(), P(), P(),
            P(None, "seq", "res"),
        ),
        out_specs=(P("seq", "res", None), P(None, "seq", "res")),
        check_vma=False,
    )
```

```python
import jax
import jax.numpy as jnp
from jax import lax
from jax.experimental import pallas as pl
from jax.experimental.pallas import tpu as pltpu
from jax.sharding import PartitionSpec as P

HEADS = 8
HD = 32
WIDTH = 256
ROWS = 1024
KEYS = 128
SEQS = 4
RES = 32
BLK = 128
CH = 256
CHUNKS = 4
F32 = jnp.float32
BF16 = jnp.bfloat16
MESH = pl.DeviceIdType.MESH
SCALE = HD ** -0.5

NN = ((1,), (0,))
NT = ((1,), (1,))
TN = ((0,), (0,))
TT = ((0,), (1,))


def dot(a, b, dims):
    return lax.dot_general(a, b, (dims, ((), ())), preferred_element_type=F32)


def loop(n, body):
    def step(i, carry):
        body(i)
        return carry
    lax.fori_loop(0, n, step, 0)


def block(i, n):
    return pl.ds(pl.multiple_of(i * n, n), n)


def kernel(
    x_ref, g_ref, wq_ref, wk_ref, wv_ref, wg_ref, wr_ref, bias_hbm,
    hom_ref, db_ref,
    bias, bias_t, mine, qa, kv, heads, gate, gated, stat, stat_in, norm, norm_in, od, od_in, dkv, dkv_out, dkv_in, total,
    bias_sem, qa_send, qa_recv, kv_send, kv_recv, st_send, st_recv, nm_send, nm_recv, od_send, od_recv, dk_send, dk_recv,
):
    a = lax.axis_index("seq")
    b = lax.axis_index("res")
    z, t = b // 8, b % 8
    cm = t // 2

    def remote(src, dst, send, recv, seq, res):
        return pltpu.make_async_remote_copy(
            src_ref=src, dst_ref=dst, send_sem=send, recv_sem=recv,
            device_id=(seq, res), device_id_type=MESH)

    def send_to(src, dst, send, recv, seq, res):
        here = jnp.logical_and(seq == a, res == b)

        @pl.when(here)
        def _():
            pltpu.make_async_copy(src, dst, recv).start()

        @pl.when(jnp.logical_not(here))
        def _():
            remote(src, dst, send, recv, seq, res).start()

    def sent(src, send, seq, res):
        here = jnp.logical_and(seq == a, res == b)

        @pl.when(jnp.logical_not(here))
        def _():
            pltpu.make_async_copy(src, src, send).wait()

    def arrived(dst, recv):
        pltpu.make_async_copy(dst, dst, recv).wait()

    def dest(i):
        c = lax.rem(cm + i // 8, CHUNKS)
        r = i % 8
        return lax.rem(z + r // 2, 4) * 8 + c * 2 + r % 2

    bias_copy = pltpu.make_async_copy(bias_hbm, bias, bias_sem)
    bias_copy.start()

    x = x_ref[...]
    mine[0] = (dot(wq_ref[...], x, TT) * SCALE).astype(BF16)
    open_gate = jax.nn.sigmoid(dot(wg_ref[...], x, TT))
    gg = dot(wr_ref[...], g_ref[...], NT)
    mine[1] = (gg * open_gate).astype(BF16)
    gate[...] = open_gate
    gated[...] = gg
    kv[a, 0] = dot(wk_ref[...], x, TT).astype(BF16)
    kv[a, 1] = dot(wv_ref[...], x, TT).astype(BF16)

    for i in range(1, 4):
        other = lax.rem(a + i, 4)
        remote(kv.at[a], kv.at[a], kv_send.at[i], kv_recv.at[a], other, b).start()

    loop(RES, lambda i: send_to(mine, qa.at[a * 8 + t], qa_send.at[i], qa_recv.at[a * 8 + t], z, dest(i)))

    bias_copy.wait()

    def turn(i):
        h, r = i // 8, block(i % 8, BLK)
        bias_t[h, :, r] = bias[h, r, :].astype(F32).T.astype(BF16)
    loop(64, turn)

    for i in range(1, 4):
        other = lax.rem(a + i, 4)
        arrived(kv.at[other], kv_recv.at[other])

    def split(i):
        s, w = i // 2, i % 2
        rows = kv[s, w].astype(F32).T.astype(BF16)
        for h in range(HEADS):
            heads[w, s, h] = rows[:, h * HD:(h + 1) * HD]
    loop(8, split)

    def chunk_of(i):
        return lax.rem(cm + CHUNKS - i, CHUNKS)

    def rows_of(ref, s, w, h, c):
        return jnp.concatenate([ref[s * 8 + c * 2 + u, w, block(h, HD), :] for u in range(2)], axis=1)

    def line_of(ref, s, row, c):
        return jnp.concatenate([ref[s * 8 + c * 2 + u, pl.ds(row, 1), :] for u in range(2)], axis=1)

    def stats_chunk(step):
        c = chunk_of(step)

        def wait(i):
            n = (i // 2) * 8 + c * 2 + i % 2
            arrived(qa.at[n], qa_recv.at[n])
        loop(8, wait)

        def head(h):
            add = bias_t[h, :, block(c, CH)].astype(F32)
            for s in range(SEQS):
                sc = dot(heads[0, s, h], rows_of(qa, s, 0, h, c), NN) + add
                top = jnp.max(sc, axis=0, keepdims=True)
                e = jnp.exp(sc - top)
                dp = dot(heads[1, s, h], rows_of(qa, s, 1, h, c), NN)
                el = jnp.sum(e, axis=0, keepdims=True)
                ed = jnp.sum(e * dp, axis=0, keepdims=True)
                for u in range(2):
                    cut = slice(u * BLK, (u + 1) * BLK)
                    n = s * 8 + c * 2 + u
                    stat[n, pl.ds(h, 1), :] = top[:, cut]
                    stat[n, pl.ds(8 + h, 1), :] = el[:, cut]
                    stat[n, pl.ds(16 + h, 1), :] = ed[:, cut]
        loop(HEADS, head)

        def ship(i):
            s, tt = i // 2, c * 2 + i % 2
            n = s * 8 + tt
            send_to(stat.at[n], stat_in.at[b], st_send.at[n], st_recv.at[b], s, a * 8 + tt)
        loop(8, ship)
    loop(CHUNKS, stats_chunk)

    loop(RES, lambda i: arrived(stat_in.at[i], st_recv.at[i]))
    top = stat_in[0, 0:8, :]
    for i in range(1, RES):
        top = jnp.maximum(top, stat_in[i, 0:8, :])
    el = jnp.zeros((8, BLK), F32)
    ed = jnp.zeros((8, BLK), F32)
    for i in range(RES):
        fix = jnp.exp(stat_in[i, 0:8, :] - top)
        el = el + stat_in[i, 8:16, :] * fix
        ed = ed + stat_in[i, 16:24, :] * fix
    norm[0:8, :] = top + jnp.log(el)
    norm[8:16, :] = ed / el
    loop(RES, lambda i: send_to(norm, norm_in.at[a * 8 + t], nm_send.at[i], nm_recv.at[a * 8 + t], z, dest(i)))

    dkv[...] = jnp.zeros_like(dkv)

    def grad_chunk(step):
        c = chunk_of(step)

        def wait(i):
            n = (i // 2) * 8 + c * 2 + i % 2
            arrived(norm_in.at[n], nm_recv.at[n])
        loop(8, wait)

        def head(h):
            hr = block(h, HD)
            add = bias_t[h, :, block(c, CH)].astype(F32)
            acc = None
            for s in range(SEQS):
                qt = rows_of(qa, s, 0, h, c)
                at = rows_of(qa, s, 1, h, c)
                p = jnp.exp(dot(heads[0, s, h], qt, NN) + add - line_of(norm_in, s, h, c))
                ds = p * (dot(heads[1, s, h], at, NN) - line_of(norm_in, s, 8 + h, c))
                acc = ds if acc is None else acc + ds
                pb = p.astype(BF16)
                sb = ds.astype(BF16)
                o = dot(kv[s, 1, hr, :], pb, NN).astype(BF16)
                dq = dot(kv[s, 0, hr, :], sb, NN).astype(BF16)
                for u in range(2):
                    n = s * 8 + c * 2 + u
                    od[n, 0, hr, :] = o[:, u * BLK:(u + 1) * BLK]
                    od[n, 1, hr, :] = dq[:, u * BLK:(u + 1) * BLK]
                dkv[s, 0, hr, :] += dot(qt, sb, NT)
                dkv[s, 1, hr, :] += dot(at, pb, NT)
            for u in range(2):
                db_ref[h, block(c * 2 + u, BLK), :] = acc[:, u * BLK:(u + 1) * BLK].T.astype(BF16)
        loop(HEADS, head)

        def ship(i):
            s, tt = i // 2, c * 2 + i % 2
            n = s * 8 + tt
            send_to(od.at[n], od_in.at[b], od_send.at[n], od_recv.at[b], s, a * 8 + tt)
        loop(8, ship)
    loop(CHUNKS, grad_chunk)

    dkv_out[...] = dkv[...].astype(BF16)
    for i in range(1, 4):
        other = lax.rem(a + i, 4)
        remote(dkv_out.at[other], dkv_in.at[a], dk_send.at[i], dk_recv.at[a], other, b).start()

    total[...] = jnp.zeros_like(total)

    def add_part(i):
        arrived(od_in.at[i], od_recv.at[i])
        total[...] += od_in[i].astype(F32)
    loop(RES, add_part)

    dkv_sum = dkv[a]
    for i in range(1, 4):
        other = lax.rem(a + i, 4)
        arrived(dkv_in.at[other], dk_recv.at[other])
        dkv_sum = dkv_sum + dkv_in[other].astype(F32)
    grads = dkv_sum.astype(BF16)
    open_gate = gate[...]
    dl = (gated[...] * total[0] * open_gate * (1.0 - open_gate)).astype(BF16)
    dq = (total[1] * SCALE).astype(BF16)
    hom = dot(dq, wq_ref[...], TT) + dot(dl, wg_ref[...], TT)
    hom = hom + dot(grads[0], wk_ref[...], TT) + dot(grads[1], wv_ref[...], TT)
    hom_ref[...] = hom.astype(BF16)

    for i in range(1, 4):
        other = lax.rem(a + i, 4)
        pltpu.make_async_copy(kv.at[a], kv.at[a], kv_send.at[i]).wait()
        pltpu.make_async_copy(dkv_out.at[other], dkv_out.at[other], dk_send.at[i]).wait()

    def finish(i):
        sent(mine, qa_send.at[i], z, dest(i))
        sent(norm, nm_send.at[i], z, dest(i))
        sent(stat.at[i], st_send.at[i], i // 8, a * 8 + i % 8)
        sent(od.at[i], od_send.at[i], i // 8, a * 8 + i % 8)
    loop(RES, finish)


def on_device(x, g, wq, wk, wv, wg, wr, bias):
    vm = pl.BlockSpec(memory_space=pltpu.VMEM)
    dma = pltpu.SemaphoreType.DMA
    hom, db = pl.pallas_call(
        kernel,
        out_shape=[
            jax.ShapeDtypeStruct((BLK, WIDTH), BF16),
            jax.ShapeDtypeStruct((HEADS, ROWS, KEYS), BF16),
        ],
        in_specs=[vm] * 7 + [pl.BlockSpec(memory_space=pl.ANY)],
        out_specs=[vm, vm],
        scratch_shapes=[
            pltpu.VMEM((HEADS, ROWS, KEYS), BF16),
            pltpu.VMEM((HEADS, KEYS, ROWS), BF16),
            pltpu.VMEM((2, WIDTH, BLK), BF16),
            pltpu.VMEM((RES, 2, WIDTH, BLK), BF16),
            pltpu.VMEM((SEQS, 2, WIDTH, KEYS), BF16),
            pltpu.VMEM((2, SEQS, HEADS, KEYS, HD), BF16),
            pltpu.VMEM((WIDTH, BLK), F32),
            pltpu.VMEM((WIDTH, BLK), F32),
            pltpu.VMEM((RES, 24, BLK), F32),
            pltpu.VMEM((RES, 24, BLK), F32),
            pltpu.VMEM((16, BLK), F32),
            pltpu.VMEM((RES, 16, BLK), F32),
            pltpu.VMEM((RES, 2, WIDTH, BLK), BF16),
            pltpu.VMEM((RES, 2, WIDTH, BLK), BF16),
            pltpu.VMEM((SEQS, 2, WIDTH, KEYS), F32),
            pltpu.VMEM((SEQS, 2, WIDTH, KEYS), BF16),
            pltpu.VMEM((SEQS, 2, WIDTH, KEYS), BF16),
            pltpu.VMEM((2, WIDTH, BLK), F32),
            dma(()),
            dma((RES,)), dma((RES,)),
            dma((SEQS,)), dma((SEQS,)),
            dma((RES,)), dma((RES,)),
            dma((RES,)), dma((RES,)),
            dma((RES,)), dma((RES,)),
            dma((SEQS,)), dma((SEQS,)),
        ],
        compiler_params=pltpu.CompilerParams(vmem_limit_bytes=56 * 2 ** 20, has_side_effects=True),
        cost_estimate=pl.CostEstimate(flops=3 * 10 ** 9, bytes_accessed=10 ** 7, transcendentals=8 * 10 ** 6),
    )(x[0], g[0], wq, wk, wv, wg, wr, bias)
    return hom[None], db.astype(F32)


def solution(mesh):
    return jax.shard_map(
        on_device,
        mesh=mesh,
        in_specs=(
            P("seq", "res", None), P("seq", "res", None), P(), P(), P(), P(), P(),
            P(None, "seq", "res"),
        ),
        out_specs=(P("seq", "res", None), P(None, "seq", "res")),
        check_vma=False,
    )
```

```python
import jax
import jax.numpy as jnp
from jax import lax
from jax.experimental import pallas as pl
from jax.experimental.pallas import tpu as pltpu
from jax.sharding import PartitionSpec as P

HEADS = 8
NH = 4
HD = 32
WIDTH = 256
HALF = 128
ROWS = 1024
KEYS = 128
SEQS = 4
BLK = 128
CH = 256
F32 = jnp.float32
BF16 = jnp.bfloat16
MESH = pl.DeviceIdType.MESH
SCALE = HD ** -0.5
ORDER = (0, 1, 3, 2)
BACK = (2, 3, 1, 0)

NN = ((1,), (0,))
NT = ((1,), (1,))
TT = ((0,), (1,))


def dot(a, b, dims):
    return lax.dot_general(a, b, (dims, ((), ())), preferred_element_type=F32)


def loop(n, body):
    def step(i, carry):
        body(i)
        return carry
    lax.fori_loop(0, n, step, 0)


def block(i, n):
    return pl.ds(pl.multiple_of(i * n, n), n)


def mod4(v):
    return lax.rem(v, 4)


def kernel(
    x_ref, g_ref, wq_ref, wk_ref, wv_ref, wg_ref, wr_ref, bias_hbm,
    hom_ref, db_hbm,
    bias_in, bias_t, mine, kvm, qa, kv, heads, gate, gated, kept, kept_pg,
    stat, stat_in, norm, norm_in, part_o, part_q, in_o, in_q, mid_o, mid_q, mid_o_in, mid_q_in,
    fin_out, fin, dkv, dkv_out, dkv_in, db_t,
    bl_sem, bs_sem, br_sem, s0_send, qa_send, qa_recv, kv_send, kv_recv, st_send, st_recv, nm_send, nm_recv,
    o1_send, o1_recv, q1_send, q1_recv, o2_send, o2_recv, q2_send, q2_recv, fin_send, fin_recv, dk_send, dk_recv,
    dl_sem, ds_sem, dr_sem,
):
    a = lax.axis_index("seq")
    b = lax.axis_index("res")
    z, xl, y = b // 8, (b // 4) % 2, b % 4
    px = 1 - xl

    def at(zz, xx, yy):
        return zz * 8 + xx * 4 + yy

    def remote(src, dst, send, recv, seq, res):
        return pltpu.make_async_remote_copy(
            src_ref=src, dst_ref=dst, send_sem=send, recv_sem=recv,
            device_id=(seq, res), device_id_type=MESH)

    def push(src, dst, send, recv, seq, res):
        here = jnp.logical_and(seq == a, res == b)

        @pl.when(here)
        def _():
            pltpu.make_async_copy(src, dst, recv).start()

        @pl.when(jnp.logical_not(here))
        def _():
            remote(src, dst, send, recv, seq, res).start()

    def pushed(src, send, seq, res):
        here = jnp.logical_and(seq == a, res == b)

        @pl.when(jnp.logical_not(here))
        def _():
            pltpu.make_async_copy(src, src, send).wait()

    def wait(ref, sem):
        pltpu.make_async_copy(ref, ref, sem).wait()

    barrier = pltpu.get_barrier_semaphore()

    def greet(seq, res):
        @pl.when(jnp.logical_not(jnp.logical_and(seq == a, res == b)))
        def _():
            pl.semaphore_signal(barrier, inc=1, device_id=(seq, res), device_id_type=MESH)

    for h in range(2):
        greet(z, at(a, h, y))
        for s in range(SEQS):
            greet(s, at(z, h, y))
    for zz in range(4):
        for yy in range(4):
            greet(a, at(zz, xl, yy))

    own_bias = pltpu.make_async_copy(bias_hbm.at[pl.ds(xl * NH, NH)], bias_in.at[xl], bl_sem)
    own_bias.start()

    x = x_ref[...]
    qt = (dot(wq_ref[...], x, TT) * SCALE).astype(BF16)
    open_gate = jax.nn.sigmoid(dot(wg_ref[...], x, TT))
    gg = dot(wr_ref[...], g_ref[...], NT)
    gt = (gg * open_gate).astype(BF16)
    gate[...] = open_gate
    gated[...] = gg
    kt = dot(wk_ref[...], x, TT).astype(BF16)
    vt = dot(wv_ref[...], x, TT).astype(BF16)
    for h in range(2):
        cut = slice(h * HALF, (h + 1) * HALF)
        mine[h, 0] = qt[cut]
        mine[h, 1] = gt[cut]
        kvm[h, 0] = kt[cut]
        kvm[h, 1] = vt[cut]

    pl.semaphore_wait(barrier, jnp.where(a == z, 23, 24))

    slot = (a * 4 + y) * 2 + xl
    for h in range(2):
        push(mine.at[h], qa.at[slot], s0_send.at[h], qa_recv.at[slot], z, at(a, h, y))
    for i in range(4):
        s = mod4(a + i)
        for h in range(2):
            push(kvm.at[h], kv.at[a * 2 + xl], kv_send.at[s * 2 + h], kv_recv.at[a * 2 + xl], s, at(z, h, y))

    def bias_piece(n):
        rows = block(n, BLK)
        return remote(
            bias_hbm.at[pl.ds(px * NH, NH), rows, :], bias_in.at[xl, :, rows, :],
            bs_sem.at[n], br_sem.at[n], a, at(z, px, y))

    def piece(z0, y0, xs):
        return (z0 * 4 + y0) * 2 + xs

    def spread(n, k, zz, yy):
        remote(qa.at[n], qa.at[n], qa_send.at[k], qa_recv.at[n], a, at(zz, xl, yy)).start()

    home = [piece(z, y, 0), piece(z, y, 1)]
    wait(qa.at[home[0]], qa_recv.at[home[0]])
    for d in (3, 1, 2):
        spread(home[0], d - 1, z, mod4(y + d))
    wait(qa.at[home[1]], qa_recv.at[home[1]])
    for d in (3, 1, 2):
        spread(home[1], 2 + d, mod4(z + d), y)
    for d in (1, 3, 2):
        spread(home[0], 5 + d, mod4(z + d), y)
    for d in (3, 1, 2):
        spread(home[1], 17 + d, z, mod4(y + d))
    for i in ORDER:
        for xs in range(2):
            bias_piece(xs * 4 + mod4(y + i)).start()

    def turn(k, h, n):
        y0, xs = n % 4, n // 4
        tile = bias_in[k, h, block(n, BLK), :]
        bias_t[h, block(k, KEYS), block(y0 * 2 + xs, BLK)] = tile.astype(F32).T.astype(BF16)

    own_bias.wait()
    loop(32, lambda i: turn(xl, i // 8, i % 8))

    for j in (1, 3, 2):
        n = piece(z, mod4(y + j), 0)
        wait(qa.at[n], qa_recv.at[n])
        for d in (1, 3, 2):
            spread(n, 5 + 3 * j + d, mod4(z + d), y)
        n = piece(mod4(z + j), y, 1)
        wait(qa.at[n], qa_recv.at[n])
        for d in (3, 1, 2):
            spread(n, 17 + 3 * j + d, z, mod4(y + d))

    for i in range(8):
        wait(kv.at[i], kv_recv.at[i])

    def split(i):
        s, k, w = i // 4, (i // 2) % 2, i % 2
        rows = kv[s * 2 + k, w].astype(F32).T.astype(BF16)
        for h in range(NH):
            heads[w, s, h, block(k, KEYS), :] = rows[:, h * HD:(h + 1) * HD]
    loop(16, split)

    def rows_of(s, w, h, y0):
        return jnp.concatenate([qa[piece(s, y0, xs), w, block(h, HD), :] for xs in range(2)], axis=1)

    for i in ORDER:
        y0 = mod4(y + i)
        cols = block(y0, CH)
        for zz in range(4):
            for xs in range(2):
                n = piece(zz, y0, xs)
                known = [jnp.logical_and(zz == z, y0 == y)]
                known.append(jnp.logical_and(xs == 0, zz == z))
                known.append(jnp.logical_and(xs == 1, y0 == y))

                @pl.when(jnp.logical_not(jnp.logical_or(known[0], jnp.logical_or(known[1], known[2]))))
                def _():
                    wait(qa.at[n], qa_recv.at[n])
        for xs in range(2):
            bias_piece(xs * 4 + y0).wait_recv()
        loop(8, lambda j: turn(px, j // 2, (j % 2) * 4 + y0))

        def stats(h):
            add = bias_t[h, :, cols].astype(F32)
            for s in range(SEQS):
                sc = dot(heads[0, s, h], rows_of(s, 0, h, y0), NN) + add
                top = jnp.max(sc, axis=0, keepdims=True)
                e = jnp.exp(sc - top)
                pg = dot(heads[1, s, h], rows_of(s, 1, h, y0), NN)
                n = s * 4 + y0
                stat[n, pl.ds(h, 1), :] = top
                stat[n, pl.ds(4 + h, 1), :] = jnp.sum(e, axis=0, keepdims=True)
                stat[n, pl.ds(8 + h, 1), :] = jnp.sum(e * pg, axis=0, keepdims=True)
                kept[s, h, :, cols] = e
                kept_pg[s, h, :, cols] = pg
        loop(NH, stats)

        for s in range(SEQS):
            n = s * 4 + y0
            push(stat.at[n], stat_in.at[z * 4 + y], st_send.at[n], st_recv.at[z * 4 + y], a, at(s, xl, y0))

    for i in range(16):
        wait(stat_in.at[i], st_recv.at[i])
    top = stat_in[0, 0:4, :]
    for i in range(1, 16):
        top = jnp.maximum(top, stat_in[i, 0:4, :])
    el = jnp.zeros((4, CH), F32)
    ed = jnp.zeros((4, CH), F32)
    for i in range(16):
        fix = jnp.exp(stat_in[i, 0:4, :] - top)
        el = el + stat_in[i, 4:8, :] * fix
        ed = ed + stat_in[i, 8:12, :] * fix
    norm[0:4, :] = top + jnp.log(el)
    norm[4:8, :] = ed / el
    for i in BACK:
        for j in range(4):
            zz, yy = mod4(z + j), mod4(y + 4 - i)
            push(norm, norm_in.at[z * 4 + y], nm_send.at[zz * 4 + yy], nm_recv.at[z * 4 + y], a, at(zz, xl, yy))

    dkv[...] = jnp.zeros_like(dkv)

    def db_own(n):
        rows = block(n, BLK)
        return pltpu.make_async_copy(
            db_t.at[xl, :, rows, :], db_hbm.at[pl.ds(xl * NH, NH), rows, :], dl_sem.at[n])

    def db_far(n):
        rows = block(n, BLK)
        return remote(
            db_t.at[px, :, rows, :], db_hbm.at[pl.ds(xl * NH, NH), rows, :],
            ds_sem.at[n], dr_sem.at[n], a, at(z, px, y))

    for i in BACK:
        y0 = mod4(y + i)
        cols = block(y0, CH)
        for s in range(SEQS):
            n = s * 4 + y0
            wait(norm_in.at[n], nm_recv.at[n])

        def grads(h):
            hr = block(h, HD)
            acc = None
            for s in range(SEQS):
                n = s * 4 + y0
                qh = rows_of(s, 0, h, y0)
                gh = rows_of(s, 1, h, y0)
                fix = jnp.exp(stat[n, pl.ds(h, 1), :] - norm_in[n, pl.ds(h, 1), :])
                p = kept[s, h, :, cols] * fix
                ds = p * (kept_pg[s, h, :, cols] - norm_in[n, pl.ds(4 + h, 1), :])
                acc = ds if acc is None else acc + ds
                pb = p.astype(BF16)
                sb = ds.astype(BF16)
                kh = jnp.concatenate([kv[s * 2 + k, 0, hr, :] for k in range(2)], axis=1)
                vh = jnp.concatenate([kv[s * 2 + k, 1, hr, :] for k in range(2)], axis=1)
                part_o[s, y0, hr, :] = dot(vh, pb, NN).astype(BF16)
                part_q[y0, s, hr, :] = dot(kh, sb, NN).astype(BF16)
                dkv[s, 0, h] += dot(sb, qh, NT)
                dkv[s, 1, h] += dot(pb, gh, NT)
            for k in range(2):
                for xs in range(2):
                    tile = acc[k * KEYS:(k + 1) * KEYS, xs * BLK:(xs + 1) * BLK]
                    db_t[k, h, block(xs * 4 + y0, BLK), :] = tile.T.astype(BF16)
        loop(NH, grads)

        for xs in range(2):
            db_far(xs * 4 + y0).start()
            db_own(xs * 4 + y0).start()
        for d in (2, 1, 3):
            zz = mod4(z + d)
            remote(part_o.at[zz, y0], in_o.at[d, y0], o1_send.at[d * 4 + i], o1_recv.at[d * 4 + y0], a, at(zz, xl, y)).start()
        if i > 0:
            remote(part_q.at[y0], in_q.at[i], q1_send.at[i], q1_recv.at[i], a, at(z, xl, y0)).start()

    for s in range(SEQS):
        for k in range(2):
            for w in range(2):
                tiles = [dkv[s, w, h, k * KEYS:(k + 1) * KEYS, :] for h in range(NH)]
                dkv_out[s * 2 + k, w] = jnp.concatenate(tiles, axis=1).astype(BF16)
    for i in range(4):
        s = mod4(a + i)
        for k in range(2):
            push(dkv_out.at[s * 2 + k], dkv_in.at[a * 2 + xl], dk_send.at[s * 2 + k], dk_recv.at[a * 2 + xl], s, at(z, k, y))

    for i in BACK:
        zz = mod4(z + i)
        if i == 2:
            for d in (1, 2, 3):
                wait(in_q.at[d], q1_recv.at[d])
        acc = part_q[y, zz].astype(F32)
        for d in (1, 2, 3):
            acc = acc + in_q[d, zz].astype(F32)
        if i > 0:
            mid_q[i] = acc.astype(BF16)
            remote(mid_q.at[i], mid_q_in.at[i], q2_send.at[i], q2_recv.at[i], a, at(zz, xl, y)).start()
        else:
            sum_q = acc
    for i in BACK:
        yy = mod4(y + i)
        acc = part_o[z, yy].astype(F32)
        for d in (1, 2, 3):
            wait(in_o.at[d, yy], o1_recv.at[d * 4 + yy])
            acc = acc + in_o[d, yy].astype(F32)
        if i > 0:
            mid_o[i] = acc.astype(BF16)
            remote(mid_o.at[i], mid_o_in.at[i], o2_send.at[i], o2_recv.at[i], a, at(z, xl, yy)).start()
        else:
            sum_o = acc
    for d in (1, 3, 2):
        wait(mid_q_in.at[d], q2_recv.at[d])
        sum_q = sum_q + mid_q_in[d].astype(F32)
    for d in (1, 3, 2):
        wait(mid_o_in.at[d], o2_recv.at[d])
        sum_o = sum_o + mid_o_in[d].astype(F32)
    for xs in range(2):
        cut = slice(xs * BLK, (xs + 1) * BLK)
        fin_out[xs, 0] = sum_o[:, cut].astype(BF16)
        fin_out[xs, 1] = sum_q[:, cut].astype(BF16)
        push(fin_out.at[xs], fin.at[xl], fin_send.at[xs], fin_recv.at[xl], z, at(a, xs, y))

    hom = jnp.zeros((BLK, WIDTH), F32)
    for i in range(8):
        wait(dkv_in.at[i], dk_recv.at[i])
    for h in range(2):
        cut = slice(h * HALF, (h + 1) * HALF)
        for w, ref in ((0, wk_ref), (1, wv_ref)):
            acc = dkv_in[h, w].astype(F32)
            for s in range(1, SEQS):
                acc = acc + dkv_in[s * 2 + h, w].astype(F32)
            hom = hom + dot(acc.astype(BF16), ref[:, cut], NT)
    for h in range(2):
        wait(fin.at[h], fin_recv.at[h])
        cut = slice(h * HALF, (h + 1) * HALF)
        og = gate[cut, :]
        dl = (gated[cut, :] * fin[h, 0].astype(F32) * og * (1.0 - og)).astype(BF16)
        dq = (fin[h, 1].astype(F32) * SCALE).astype(BF16)
        hom = hom + dot(dq, wq_ref[:, cut], TT) + dot(dl, wg_ref[:, cut], TT)
    hom_ref[...] = hom.astype(BF16)

    for h in range(2):
        pushed(mine.at[h], s0_send.at[h], z, at(a, h, y))
        pushed(fin_out.at[h], fin_send.at[h], z, at(a, h, y))
        for s in range(SEQS):
            pushed(kvm.at[h], kv_send.at[s * 2 + h], s, at(z, h, y))
            pushed(dkv_out.at[s * 2 + h], dk_send.at[s * 2 + h], s, at(z, h, y))
    for k in range(30):
        wait(qa.at[0], qa_send.at[k])
    for n in range(16):
        pushed(stat.at[n], st_send.at[n], a, at(n // 4, xl, n % 4))
        pushed(norm, nm_send.at[n], a, at(n // 4, xl, n % 4))
    for d in (1, 2, 3):
        for i in range(4):
            wait(part_o.at[0, 0], o1_send.at[d * 4 + i])
        wait(part_q.at[0], q1_send.at[d])
        wait(mid_o.at[d], o2_send.at[d])
        wait(mid_q.at[d], q2_send.at[d])
    for n in range(8):
        bias_piece(n).wait_send()
        db_own(n).wait()
        db_far(n).wait()


def on_device(x, g, wq, wk, wv, wg, wr, bias):
    vm = pl.BlockSpec(memory_space=pltpu.VMEM)
    hbm = pl.BlockSpec(memory_space=pl.ANY)
    dma = pltpu.SemaphoreType.DMA
    V = pltpu.VMEM
    hom, db = pl.pallas_call(
        kernel,
        out_shape=[
            jax.ShapeDtypeStruct((BLK, WIDTH), BF16),
            jax.ShapeDtypeStruct((HEADS, ROWS, KEYS), BF16),
        ],
        in_specs=[vm] * 7 + [hbm],
        out_specs=[vm, hbm],
        scratch_shapes=[
            V((2, NH, ROWS, KEYS), BF16),
            V((NH, 2 * KEYS, ROWS), BF16),
            V((2, 2, HALF, BLK), BF16),
            V((2, 2, HALF, BLK), BF16),
            V((32, 2, HALF, BLK), BF16),
            V((8, 2, HALF, KEYS), BF16),
            V((2, SEQS, NH, 2 * KEYS, HD), BF16),
            V((WIDTH, BLK), F32),
            V((WIDTH, BLK), F32),
            V((SEQS, NH, 2 * KEYS, ROWS), F32),
            V((SEQS, NH, 2 * KEYS, ROWS), F32),
            V((16, 16, CH), F32),
            V((16, 16, CH), F32),
            V((8, CH), F32),
            V((16, 8, CH), F32),
            V((4, 4, HALF, CH), BF16),
            V((4, 4, HALF, CH), BF16),
            V((4, 4, HALF, CH), BF16),
            V((4, 4, HALF, CH), BF16),
            V((4, HALF, CH), BF16),
            V((4, HALF, CH), BF16),
            V((4, HALF, CH), BF16),
            V((4, HALF, CH), BF16),
            V((2, 2, HALF, BLK), BF16),
            V((2, 2, HALF, BLK), BF16),
            V((SEQS, 2, NH, 2 * KEYS, HD), F32),
            V((8, 2, KEYS, HALF), BF16),
            V((8, 2, KEYS, HALF), BF16),
            V((2, NH, ROWS, KEYS), BF16),
            dma(()), dma((8,)), dma((8,)),
            dma((2,)), dma((30,)), dma((32,)),
            dma((8,)), dma((8,)),
            dma((16,)), dma((16,)),
            dma((16,)), dma((16,)),
            dma((16,)), dma((16,)),
            dma((4,)), dma((4,)),
            dma((4,)), dma((4,)),
            dma((4,)), dma((4,)),
            dma((2,)), dma((2,)),
            dma((8,)), dma((8,)),
            dma((8,)), dma((8,)), dma((8,)),
        ],
        compiler_params=pltpu.CompilerParams(
            vmem_limit_bytes=60 * 2 ** 20, has_side_effects=True, collective_id=0),
        cost_estimate=pl.CostEstimate(flops=3 * 10 ** 9, bytes_accessed=10 ** 7, transcendentals=8 * 10 ** 6),
    )(x[0], g[0], wq, wk, wv, wg, wr, bias)
    return hom[None], db.astype(F32)


def solution(mesh):
    return jax.shard_map(
        on_device,
        mesh=mesh,
        in_specs=(
            P("seq", "res", None), P("seq", "res", None), P(), P(), P(), P(), P(),
            P(None, "seq", "res"),
        ),
        out_specs=(P("seq", "res", None), P(None, "seq", "res")),
        check_vma=False,
    )
```

```python
import jax
import jax.numpy as jnp
from jax import lax
from jax.experimental import pallas as pl
from jax.experimental.pallas import tpu as pltpu
from jax.sharding import PartitionSpec as P

HEADS = 8
NH = 4
GROUPS = 2
GH = 2
GW = 64
HD = 32
WIDTH = 256
HALF = 128
ROWS = 1024
KEYS = 128
SEQS = 4
BLK = 128
CH = 256
F32 = jnp.float32
BF16 = jnp.bfloat16
MESH = pl.DeviceIdType.MESH
SCALE = HD ** -0.5
ORDER = (0, 1, 3, 2)
BACK = (2, 3, 1, 0)

NN = ((1,), (0,))
NT = ((1,), (1,))
TT = ((0,), (1,))


def dot(a, b, dims):
    return lax.dot_general(a, b, (dims, ((), ())), preferred_element_type=F32)


def loop(n, body):
    def step(i, carry):
        body(i)
        return carry
    lax.fori_loop(0, n, step, 0)


def block(i, n):
    return pl.ds(pl.multiple_of(i * n, n), n)


def mod4(v):
    return lax.rem(v, 4)


def kernel(
    x_ref, g_ref, wq_ref, wk_ref, wv_ref, wg_ref, wr_ref, bias_hbm,
    hom_ref, db_hbm,
    bias_in, bias_t, mine, kvm, qa, kv, heads, gate, gated, kept, kept_pg,
    stat, stat_in, norm, norm_in, part_o, part_q, in_o, in_q, mid_o, mid_q, mid_o_in, mid_q_in,
    fin_out, fin, dkv, dkv_out, dkv_mid, dkv_sum, dkv_in, db_t,
    bl_sem, bs_sem, br_sem, s0_send, qa_send, qa_recv, kv_send, kv_recv, kr_send, st_send, st_recv, nm_send, nm_recv,
    o1_send, o1_recv, q1_send, q1_recv, o2_send, o2_recv, q2_send, q2_recv, fin_send, fin_recv,
    dm_send, dm_recv, dk_send, dk_recv, dl_sem, ds_sem, dr_sem,
):
    a = lax.axis_index("seq")
    b = lax.axis_index("res")
    z, xl, y = b // 8, (b // 4) % 2, b % 4
    px = 1 - xl
    xh, co = a // 2, a % 2
    twin = a + 1 - 2 * co

    def at(zz, xx, yy):
        return zz * 8 + xx * 4 + yy

    def remote(src, dst, send, recv, seq, res):
        return pltpu.make_async_remote_copy(
            src_ref=src, dst_ref=dst, send_sem=send, recv_sem=recv,
            device_id=(seq, res), device_id_type=MESH)

    def push(src, dst, send, recv, seq, res):
        here = jnp.logical_and(seq == a, res == b)

        @pl.when(here)
        def _():
            pltpu.make_async_copy(src, dst, recv).start()

        @pl.when(jnp.logical_not(here))
        def _():
            remote(src, dst, send, recv, seq, res).start()

    def pushed(src, send, seq, res):
        here = jnp.logical_and(seq == a, res == b)

        @pl.when(jnp.logical_not(here))
        def _():
            pltpu.make_async_copy(src, src, send).wait()

    def wait(ref, sem):
        pltpu.make_async_copy(ref, ref, sem).wait()

    barrier = pltpu.get_barrier_semaphore()

    def greet(seq, res):
        @pl.when(jnp.logical_not(jnp.logical_and(seq == a, res == b)))
        def _():
            pl.semaphore_signal(barrier, inc=1, device_id=(seq, res), device_id_type=MESH)

    for h in range(2):
        greet(z, at(a, h, y))
        for s in range(2):
            greet(s * 2 + co, at(z, h, y))
    greet(twin, b)
    for zz in range(4):
        for yy in range(4):
            greet(a, at(zz, xl, yy))

    own_bias = pltpu.make_async_copy(bias_hbm.at[pl.ds(xl * NH, NH)], bias_in.at[xl], bl_sem)
    own_bias.start()

    x = x_ref[...]
    qt = (dot(wq_ref[...], x, TT) * SCALE).astype(BF16)
    open_gate = jax.nn.sigmoid(dot(wg_ref[...], x, TT))
    gg = dot(wr_ref[...], g_ref[...], NT)
    gt = (gg * open_gate).astype(BF16)
    gate[...] = open_gate
    gated[...] = gg
    kt = dot(wk_ref[...], x, TT).astype(BF16)
    vt = dot(wv_ref[...], x, TT).astype(BF16)
    for h in range(2):
        for g in range(GROUPS):
            cut = slice(h * HALF + g * GW, h * HALF + (g + 1) * GW)
            mine[h, g, 0] = qt[cut]
            mine[h, g, 1] = gt[cut]
        cut = slice(h * HALF, (h + 1) * HALF)
        kvm[h, 0] = kt[cut]
        kvm[h, 1] = vt[cut]

    pl.semaphore_wait(barrier, jnp.where(a == z, 20, 21))

    slot = (a * 4 + y) * 2 + xl
    for g in range(GROUPS):
        for h in range(2):
            push(mine.at[h, g], qa.at[slot, g], s0_send.at[g * 2 + h], qa_recv.at[g * 32 + slot], z, at(a, h, y))
    for i in range(2):
        s = lax.rem(xh + i, 2)
        for h in range(2):
            push(kvm.at[h], kv.at[a * 2 + xl], kv_send.at[s * 2 + h], kv_recv.at[a * 2 + xl], s * 2 + co, at(z, h, y))

    def bias_piece(g, n):
        rows = block(n, BLK)
        return remote(
            bias_hbm.at[pl.ds(px * NH + g * GH, GH), rows, :], bias_in.at[xl, pl.ds(g * GH, GH), rows, :],
            bs_sem.at[g * 8 + n], br_sem.at[g * 8 + n], a, at(z, px, y))

    def bias_send(g):
        for i in ORDER:
            for xs in range(2):
                bias_piece(g, xs * 4 + mod4(y + i)).start()

    def piece(z0, y0, xs):
        return (z0 * 4 + y0) * 2 + xs

    def landed(g, n):
        wait(qa.at[n, g], qa_recv.at[g * 32 + n])

    def spread(g, n, k, zz, yy):
        remote(qa.at[n, g], qa.at[n, g], qa_send.at[g * 30 + k], qa_recv.at[g * 32 + n], a, at(zz, xl, yy)).start()

    bias_send(0)
    home = [piece(z, y, 0), piece(z, y, 1)]
    for g in range(GROUPS):
        landed(g, home[0])
        for d in (3, 1, 2):
            spread(g, home[0], d - 1, z, mod4(y + d))
        landed(g, home[1])
        for d in (3, 1, 2):
            spread(g, home[1], 2 + d, mod4(z + d), y)
        for d in (1, 3, 2):
            spread(g, home[0], 5 + d, mod4(z + d), y)
        for d in (3, 1, 2):
            spread(g, home[1], 17 + d, z, mod4(y + d))
    bias_send(1)

    def turn(k, h, n):
        y0, xs = n % 4, n // 4
        tile = bias_in[k, h, block(n, BLK), :]
        bias_t[h, block(k, KEYS), block(y0 * 2 + xs, BLK)] = tile.astype(F32).T.astype(BF16)

    own_bias.wait()
    loop(32, lambda i: turn(xl, i // 8, i % 8))

    for i in range(2):
        for k in range(2):
            n = (i * 2 + co) * 2 + k
            wait(kv.at[n], kv_recv.at[n])
            remote(kv.at[n], kv.at[n], kr_send.at[i * 2 + k], kv_recv.at[n], twin, b).start()

    for g in range(GROUPS):
        for j in (1, 3, 2):
            n = piece(z, mod4(y + j), 0)
            landed(g, n)
            for d in (1, 3, 2):
                spread(g, n, 5 + 3 * j + d, mod4(z + d), y)
            n = piece(mod4(z + j), y, 1)
            landed(g, n)
            for d in (3, 1, 2):
                spread(g, n, 17 + 3 * j + d, z, mod4(y + d))

    for i in range(2):
        for k in range(2):
            n = (i * 2 + 1 - co) * 2 + k
            wait(kv.at[n], kv_recv.at[n])

    def split(i):
        s, k, w = i // 4, (i // 2) % 2, i % 2
        rows = kv[s * 2 + k, w].astype(F32).T.astype(BF16)
        for h in range(NH):
            heads[w, s, h, block(k, KEYS), :] = rows[:, h * HD:(h + 1) * HD]
    loop(16, split)

    def rows_of(s, w, g, hh, y0):
        return jnp.concatenate([qa[piece(s, y0, xs), g, w, block(hh, HD), :] for xs in range(2)], axis=1)

    def stats_group(g):
        for i in ORDER:
            y0 = mod4(y + i)
            cols = block(y0, CH)
            if i > 0:
                for d in (1, 2, 3):
                    landed(g, piece(mod4(z + d), y0, 0))
                for d in range(4):
                    landed(g, piece(mod4(z + d), y0, 1))
            else:
                for d in (1, 2, 3):
                    landed(g, piece(mod4(z + d), y0, 0))
            for xs in range(2):
                bias_piece(g, xs * 4 + y0).wait_recv()
            loop(2 * GH, lambda j: turn(px, g * GH + j // 2, (j % 2) * 4 + y0))

            def stats(hh):
                h = g * GH + hh
                add = bias_t[h, :, cols].astype(F32)
                for s in range(SEQS):
                    sc = dot(heads[0, s, h], rows_of(s, 0, g, hh, y0), NN) + add
                    top = jnp.max(sc, axis=0, keepdims=True)
                    e = jnp.exp(sc - top)
                    pg = dot(heads[1, s, h], rows_of(s, 1, g, hh, y0), NN)
                    n = s * 4 + y0
                    stat[g, n, pl.ds(hh, 1), :] = top
                    stat[g, n, pl.ds(2 + hh, 1), :] = jnp.sum(e, axis=0, keepdims=True)
                    stat[g, n, pl.ds(4 + hh, 1), :] = jnp.sum(e * pg, axis=0, keepdims=True)
                    kept[s, h, :, cols] = e
                    kept_pg[s, h, :, cols] = pg
            loop(GH, stats)

            for s in range(SEQS):
                n = s * 4 + y0
                push(stat.at[g, n], stat_in.at[g, z * 4 + y], st_send.at[g * 16 + n],
                     st_recv.at[g * 16 + z * 4 + y], a, at(s, xl, y0))

    def combine(g):
        for i in range(16):
            wait(stat_in.at[g, i], st_recv.at[g * 16 + i])
        top = stat_in[g, 0, 0:2, :]
        for i in range(1, 16):
            top = jnp.maximum(top, stat_in[g, i, 0:2, :])
        el = jnp.zeros((2, CH), F32)
        ed = jnp.zeros((2, CH), F32)
        for i in range(16):
            fix = jnp.exp(stat_in[g, i, 0:2, :] - top)
            el = el + stat_in[g, i, 2:4, :] * fix
            ed = ed + stat_in[g, i, 4:6, :] * fix
        norm[g, 0:2, :] = top + jnp.log(el)
        norm[g, 2:4, :] = ed / el
        for i in BACK:
            for j in range(4):
                zz, yy = mod4(z + j), mod4(y + 4 - i)
                push(norm.at[g], norm_in.at[g, z * 4 + y], nm_send.at[g * 16 + zz * 4 + yy],
                     nm_recv.at[g * 16 + z * 4 + y], a, at(zz, xl, yy))

    def db_own(g, n):
        rows = block(n, BLK)
        return pltpu.make_async_copy(
            db_t.at[xl, pl.ds(g * GH, GH), rows, :], db_hbm.at[pl.ds(xl * NH + g * GH, GH), rows, :], dl_sem.at[g * 8 + n])

    def db_far(g, n):
        rows = block(n, BLK)
        return remote(
            db_t.at[px, pl.ds(g * GH, GH), rows, :], db_hbm.at[pl.ds(xl * NH + g * GH, GH), rows, :],
            ds_sem.at[g * 8 + n], dr_sem.at[g * 8 + n], a, at(z, px, y))

    def grads_group(g):
        for i in BACK:
            y0 = mod4(y + i)
            cols = block(y0, CH)
            for s in range(SEQS):
                n = s * 4 + y0
                wait(norm_in.at[g, n], nm_recv.at[g * 16 + n])

            def grads(hh):
                h = g * GH + hh
                hr = block(h, HD)
                gr = block(hh, HD)
                acc = None
                for s in range(SEQS):
                    n = s * 4 + y0
                    qh = rows_of(s, 0, g, hh, y0)
                    gh = rows_of(s, 1, g, hh, y0)
                    fix = jnp.exp(stat[g, n, pl.ds(hh, 1), :] - norm_in[g, n, pl.ds(hh, 1), :])
                    p = kept[s, h, :, cols] * fix
                    ds = p * (kept_pg[s, h, :, cols] - norm_in[g, n, pl.ds(2 + hh, 1), :])
                    acc = ds if acc is None else acc + ds
                    pb = p.astype(BF16)
                    sb = ds.astype(BF16)
                    kh = jnp.concatenate([kv[s * 2 + k, 0, hr, :] for k in range(2)], axis=1)
                    vh = jnp.concatenate([kv[s * 2 + k, 1, hr, :] for k in range(2)], axis=1)
                    part_o[g, s, y0, gr, :] = dot(vh, pb, NN).astype(BF16)
                    part_q[y0, g, s, gr, :] = dot(kh, sb, NN).astype(BF16)
                    dkv[s, 0, h] += dot(sb, qh, NT)
                    dkv[s, 1, h] += dot(pb, gh, NT)
                for k in range(2):
                    for xs in range(2):
                        tile = acc[k * KEYS:(k + 1) * KEYS, xs * BLK:(xs + 1) * BLK]
                        db_t[k, h, block(xs * 4 + y0, BLK), :] = tile.T.astype(BF16)
            loop(GH, grads)

            for xs in range(2):
                db_far(g, xs * 4 + y0).start()
                db_own(g, xs * 4 + y0).start()
            for d in (2, 1, 3):
                zz = mod4(z + d)
                remote(part_o.at[g, zz, y0], in_o.at[g, d, y0], o1_send.at[g * 16 + d * 4 + i],
                       o1_recv.at[g * 16 + d * 4 + y0], a, at(zz, xl, y)).start()
            if i > 0:
                remote(part_q.at[y0, g], in_q.at[i, g], q1_send.at[g * 4 + i], q1_recv.at[g * 4 + i], a, at(z, xl, y0)).start()

        for s in range(SEQS):
            for k in range(2):
                tiles = [dkv[s, w, g * GH + hh, k * KEYS:(k + 1) * KEYS, :] for w in range(2) for hh in range(GH)]
                dkv_out[g, s * 2 + k] = jnp.concatenate(tiles, axis=1).astype(BF16)
        for i in range(2):
            for k in range(2):
                remote(dkv_out.at[g, (i * 2 + 1 - co) * 2 + k], dkv_mid.at[g, i * 2 + k],
                       dm_send.at[g * 4 + i * 2 + k], dm_recv.at[g * 4 + i * 2 + k], twin, b).start()

    def key_grads(g):
        for j in range(2):
            i = lax.rem(xh + 1 + j, 2)
            for k in range(2):
                n = i * 2 + k
                wait(dkv_mid.at[g, n], dm_recv.at[g * 4 + n])
                both = dkv_out[g, (i * 2 + co) * 2 + k].astype(F32) + dkv_mid[g, n].astype(F32)
                dkv_sum[g, n] = both.astype(BF16)
                push(dkv_sum.at[g, n], dkv_in.at[g, xh * 2 + xl], dk_send.at[g * 4 + n],
                     dk_recv.at[g * 4 + xh * 2 + xl], i * 2 + co, at(z, k, y))

    dkv[...] = jnp.zeros_like(dkv)
    stats_group(0)
    combine(0)
    stats_group(1)
    grads_group(0)
    combine(1)
    key_grads(0)
    grads_group(1)
    key_grads(1)

    for g in range(GROUPS):
        for d in (1, 2, 3):
            wait(in_q.at[d, g], q1_recv.at[g * 4 + d])
    for i in BACK:
        zz = mod4(z + i)
        accs = []
        for g in range(GROUPS):
            acc = part_q[y, g, zz].astype(F32)
            for d in (1, 2, 3):
                acc = acc + in_q[d, g, zz].astype(F32)
            accs.append(acc)
        acc = jnp.concatenate(accs, axis=0)
        if i > 0:
            mid_q[i] = acc.astype(BF16)
            remote(mid_q.at[i], mid_q_in.at[i], q2_send.at[i], q2_recv.at[i], a, at(zz, xl, y)).start()
        else:
            sum_q = acc
    for i in BACK:
        yy = mod4(y + i)
        accs = []
        for g in range(GROUPS):
            acc = part_o[g, z, yy].astype(F32)
            for d in (1, 2, 3):
                wait(in_o.at[g, d, yy], o1_recv.at[g * 16 + d * 4 + yy])
                acc = acc + in_o[g, d, yy].astype(F32)
            accs.append(acc)
        acc = jnp.concatenate(accs, axis=0)
        if i > 0:
            mid_o[i] = acc.astype(BF16)
            remote(mid_o.at[i], mid_o_in.at[i], o2_send.at[i], o2_recv.at[i], a, at(z, xl, yy)).start()
        else:
            sum_o = acc
    for d in (1, 3, 2):
        wait(mid_q_in.at[d], q2_recv.at[d])
        sum_q = sum_q + mid_q_in[d].astype(F32)
    for d in (1, 3, 2):
        wait(mid_o_in.at[d], o2_recv.at[d])
        sum_o = sum_o + mid_o_in[d].astype(F32)
    for xs in range(2):
        cut = slice(xs * BLK, (xs + 1) * BLK)
        fin_out[xs, 0] = sum_o[:, cut].astype(BF16)
        fin_out[xs, 1] = sum_q[:, cut].astype(BF16)
        push(fin_out.at[xs], fin.at[xl], fin_send.at[xs], fin_recv.at[xl], z, at(a, xs, y))

    hom = jnp.zeros((BLK, WIDTH), F32)
    for g in range(GROUPS):
        for i in range(4):
            wait(dkv_in.at[g, i], dk_recv.at[g * 4 + i])
        for h in range(2):
            acc = (dkv_in[g, h].astype(F32) + dkv_in[g, 2 + h].astype(F32)).astype(BF16)
            cut = slice(h * HALF + g * GW, h * HALF + (g + 1) * GW)
            hom = hom + dot(acc[:, :GW], wk_ref[:, cut], NT) + dot(acc[:, GW:], wv_ref[:, cut], NT)
    for h in range(2):
        wait(fin.at[h], fin_recv.at[h])
        cut = slice(h * HALF, (h + 1) * HALF)
        og = gate[cut, :]
        dl = (gated[cut, :] * fin[h, 0].astype(F32) * og * (1.0 - og)).astype(BF16)
        dq = (fin[h, 1].astype(F32) * SCALE).astype(BF16)
        hom = hom + dot(dq, wq_ref[:, cut], TT) + dot(dl, wg_ref[:, cut], TT)
    hom_ref[...] = hom.astype(BF16)

    for h in range(2):
        pushed(fin_out.at[h], fin_send.at[h], z, at(a, h, y))
        for s in range(2):
            pushed(kvm.at[h], kv_send.at[s * 2 + h], s * 2 + co, at(z, h, y))
            wait(kv.at[0], kr_send.at[s * 2 + h])
    for g in range(GROUPS):
        for h in range(2):
            pushed(mine.at[h, g], s0_send.at[g * 2 + h], z, at(a, h, y))
            for s in range(2):
                n = s * 2 + h
                wait(dkv_mid.at[g, n], dm_send.at[g * 4 + n])
                pushed(dkv_sum.at[g, n], dk_send.at[g * 4 + n], s * 2 + co, at(z, h, y))
        for k in range(30):
            wait(qa.at[0, g], qa_send.at[g * 30 + k])
        for n in range(16):
            pushed(stat.at[g, n], st_send.at[g * 16 + n], a, at(n // 4, xl, n % 4))
            pushed(norm.at[g], nm_send.at[g * 16 + n], a, at(n // 4, xl, n % 4))
        for d in (1, 2, 3):
            for i in range(4):
                wait(part_o.at[g, 0, 0], o1_send.at[g * 16 + d * 4 + i])
            wait(part_q.at[0, g], q1_send.at[g * 4 + d])
        for n in range(8):
            bias_piece(g, n).wait_send()
            db_own(g, n).wait()
            db_far(g, n).wait()
    for d in (1, 2, 3):
        wait(mid_o.at[d], o2_send.at[d])
        wait(mid_q.at[d], q2_send.at[d])


def on_device(x, g, wq, wk, wv, wg, wr, bias):
    vm = pl.BlockSpec(memory_space=pltpu.VMEM)
    hbm = pl.BlockSpec(memory_space=pl.ANY)
    dma = pltpu.SemaphoreType.DMA
    V = pltpu.VMEM
    hom, db = pl.pallas_call(
        kernel,
        out_shape=[
            jax.ShapeDtypeStruct((BLK, WIDTH), BF16),
            jax.ShapeDtypeStruct((HEADS, ROWS, KEYS), BF16),
        ],
        in_specs=[vm] * 7 + [hbm],
        out_specs=[vm, hbm],
        scratch_shapes=[
            V((2, NH, ROWS, KEYS), BF16),
            V((NH, 2 * KEYS, ROWS), BF16),
            V((2, GROUPS, 2, GW, BLK), BF16),
            V((2, 2, HALF, BLK), BF16),
            V((32, GROUPS, 2, GW, BLK), BF16),
            V((8, 2, HALF, KEYS), BF16),
            V((2, SEQS, NH, 2 * KEYS, HD), BF16),
            V((WIDTH, BLK), F32),
            V((WIDTH, BLK), F32),
            V((SEQS, NH, 2 * KEYS, ROWS), F32),
            V((SEQS, NH, 2 * KEYS, ROWS), F32),
            V((GROUPS, 16, 8, CH), F32),
            V((GROUPS, 16, 8, CH), F32),
            V((GROUPS, 8, CH), F32),
            V((GROUPS, 16, 8, CH), F32),
            V((GROUPS, 4, 4, GW, CH), BF16),
            V((4, GROUPS, 4, GW, CH), BF16),
            V((GROUPS, 4, 4, GW, CH), BF16),
            V((4, GROUPS, 4, GW, CH), BF16),
            V((4, HALF, CH), BF16),
            V((4, HALF, CH), BF16),
            V((4, HALF, CH), BF16),
            V((4, HALF, CH), BF16),
            V((2, 2, HALF, BLK), BF16),
            V((2, 2, HALF, BLK), BF16),
            V((SEQS, 2, NH, 2 * KEYS, HD), F32),
            V((GROUPS, 8, KEYS, HALF), BF16),
            V((GROUPS, 4, KEYS, HALF), BF16),
            V((GROUPS, 4, KEYS, HALF), BF16),
            V((GROUPS, 4, KEYS, HALF), BF16),
            V((2, NH, ROWS, KEYS), BF16),
            dma(()), dma((16,)), dma((16,)),
            dma((4,)), dma((60,)), dma((64,)),
            dma((4,)), dma((8,)), dma((4,)),
            dma((32,)), dma((32,)),
            dma((32,)), dma((32,)),
            dma((32,)), dma((32,)),
            dma((8,)), dma((8,)),
            dma((4,)), dma((4,)),
            dma((4,)), dma((4,)),
            dma((2,)), dma((2,)),
            dma((8,)), dma((8,)),
            dma((8,)), dma((8,)),
            dma((16,)), dma((16,)), dma((16,)),
        ],
        compiler_params=pltpu.CompilerParams(
            vmem_limit_bytes=60 * 2 ** 20, has_side_effects=True, collective_id=0),
        cost_estimate=pl.CostEstimate(flops=3 * 10 ** 9, bytes_accessed=10 ** 7, transcendentals=8 * 10 ** 6),
    )(x[0], g[0], wq, wk, wv, wg, wr, bias)
    return hom[None], db.astype(F32)


def solution(mesh):
    return jax.shard_map(
        on_device,
        mesh=mesh,
        in_specs=(
            P("seq", "res", None), P("seq", "res", None), P(), P(), P(), P(), P(),
            P(None, "seq", "res"),
        ),
        out_specs=(P("seq", "res", None), P(None, "seq", "res")),
        check_vma=False,
    )
```

```python
import jax
import jax.numpy as jnp
from jax import lax
from jax.experimental import pallas as pl
from jax.experimental.pallas import tpu as pltpu
from jax.sharding import PartitionSpec as P

HEADS = 8
NH = 4
GROUPS = 2
GH = 2
GW = 64
HD = 32
WIDTH = 256
HALF = 128
ROWS = 1024
KEYS = 128
SEQS = 4
BLK = 128
CH = 256
F32 = jnp.float32
BF16 = jnp.bfloat16
MESH = pl.DeviceIdType.MESH
SCALE = HD ** -0.5
ORDER = (0, 1, 3, 2)
BACK = (2, 3, 1, 0)

NN = ((1,), (0,))
NT = ((1,), (1,))
TT = ((0,), (1,))


def dot(a, b, dims):
    return lax.dot_general(a, b, (dims, ((), ())), preferred_element_type=F32)


def loop(n, body):
    def step(i, carry):
        body(i)
        return carry
    lax.fori_loop(0, n, step, 0)


def block(i, n):
    return pl.ds(pl.multiple_of(i * n, n), n)


def mod4(v):
    return lax.rem(v, 4)


def kernel(
    x_ref, g_ref, wq_ref, wk_ref, wv_ref, wg_ref, wr_ref, bias_hbm,
    hom_ref, db_hbm,
    bias_in, eye, mine, kvm, qa, kv, heads, gate, gated, kept, kept_pg,
    stat, stat_in, norm, norm_in, part_o, part_q, in_o, in_q, mid_o, mid_q, mid_o_in, mid_q_in,
    fin_out, fin, dkv, dkv_out, dkv_mid, dkv_sum, dkv_in, db_t,
    bl_sem, bs_sem, br_sem, s0_send, qa_send, qa_recv, kv_send, kv_recv, kr_send, st_send, st_recv, nm_send, nm_recv,
    o1_send, o1_recv, q1_send, q1_recv, o2_send, o2_recv, q2_send, q2_recv, fin_send, fin_recv,
    dm_send, dm_recv, dk_send, dk_recv, dl_sem, ds_sem, dr_sem,
):
    a = lax.axis_index("seq")
    b = lax.axis_index("res")
    z, xl, y = b // 8, (b // 4) % 2, b % 4
    px = 1 - xl
    xh, co = a // 2, a % 2
    twin = a + 1 - 2 * co

    def at(zz, xx, yy):
        return zz * 8 + xx * 4 + yy

    def remote(src, dst, send, recv, seq, res):
        return pltpu.make_async_remote_copy(
            src_ref=src, dst_ref=dst, send_sem=send, recv_sem=recv,
            device_id=(seq, res), device_id_type=MESH)

    def push(src, dst, send, recv, seq, res):
        here = jnp.logical_and(seq == a, res == b)

        @pl.when(here)
        def _():
            pltpu.make_async_copy(src, dst, recv).start()

        @pl.when(jnp.logical_not(here))
        def _():
            remote(src, dst, send, recv, seq, res).start()

    def pushed(src, send, seq, res):
        here = jnp.logical_and(seq == a, res == b)

        @pl.when(jnp.logical_not(here))
        def _():
            pltpu.make_async_copy(src, src, send).wait()

    def wait(ref, sem):
        pltpu.make_async_copy(ref, ref, sem).wait()

    barrier = pltpu.get_barrier_semaphore()

    def greet(seq, res):
        @pl.when(jnp.logical_not(jnp.logical_and(seq == a, res == b)))
        def _():
            pl.semaphore_signal(barrier, inc=1, device_id=(seq, res), device_id_type=MESH)

    for h in range(2):
        greet(z, at(a, h, y))
        for s in range(2):
            greet(s * 2 + co, at(z, h, y))
    greet(twin, b)
    for zz in range(4):
        for yy in range(4):
            greet(a, at(zz, xl, yy))

    own_bias = pltpu.make_async_copy(bias_hbm.at[pl.ds(xl * NH, NH)], bias_in.at[xl], bl_sem)
    own_bias.start()

    same = lax.broadcasted_iota(jnp.int32, (KEYS, KEYS), 0) == lax.broadcasted_iota(jnp.int32, (KEYS, KEYS), 1)
    eye[...] = jnp.where(same, 1.0, 0.0).astype(BF16)

    x = x_ref[...]
    qt = (dot(wq_ref[...], x, TT) * SCALE).astype(BF16)
    open_gate = jax.nn.sigmoid(dot(wg_ref[...], x, TT))
    gg = dot(wr_ref[...], g_ref[...], NT)
    gt = (gg * open_gate).astype(BF16)
    gate[...] = open_gate
    gated[...] = gg
    kt = dot(wk_ref[...], x, TT).astype(BF16)
    vt = dot(wv_ref[...], x, TT).astype(BF16)
    for h in range(2):
        for g in range(GROUPS):
            cut = slice(h * HALF + g * GW, h * HALF + (g + 1) * GW)
            mine[h, g, 0] = qt[cut]
            mine[h, g, 1] = gt[cut]
        cut = slice(h * HALF, (h + 1) * HALF)
        kvm[h, 0] = kt[cut]
        kvm[h, 1] = vt[cut]

    pl.semaphore_wait(barrier, jnp.where(a == z, 20, 21))

    slot = (a * 4 + y) * 2 + xl
    for g in range(GROUPS):
        for h in range(2):
            push(mine.at[h, g], qa.at[slot, g], s0_send.at[g * 2 + h], qa_recv.at[g * 32 + slot], z, at(a, h, y))
    for i in range(2):
        s = lax.rem(xh + i, 2)
        for h in range(2):
            push(kvm.at[h], kv.at[a * 2 + xl], kv_send.at[s * 2 + h], kv_recv.at[a * 2 + xl], s * 2 + co, at(z, h, y))

    def bias_piece(g, n):
        rows = block(n, BLK)
        return remote(
            bias_hbm.at[pl.ds(px * NH + g * GH, GH), rows, :], bias_in.at[xl, pl.ds(g * GH, GH), rows, :],
            bs_sem.at[g * 8 + n], br_sem.at[g * 8 + n], a, at(z, px, y))

    def bias_send(g):
        for i in ORDER:
            for xs in range(2):
                bias_piece(g, xs * 4 + mod4(y + i)).start()

    def piece(z0, y0, xs):
        return (z0 * 4 + y0) * 2 + xs

    def landed(g, n):
        wait(qa.at[n, g], qa_recv.at[g * 32 + n])

    def spread(g, n, k, zz, yy):
        remote(qa.at[n, g], qa.at[n, g], qa_send.at[g * 30 + k], qa_recv.at[g * 32 + n], a, at(zz, xl, yy)).start()

    bias_send(0)
    home = [piece(z, y, 0), piece(z, y, 1)]
    for g in range(GROUPS):
        landed(g, home[0])
        for d in (3, 1, 2):
            spread(g, home[0], d - 1, z, mod4(y + d))
        landed(g, home[1])
        for d in (3, 1, 2):
            spread(g, home[1], 2 + d, mod4(z + d), y)
        for d in (1, 3, 2):
            spread(g, home[0], 5 + d, mod4(z + d), y)
        for d in (3, 1, 2):
            spread(g, home[1], 17 + d, z, mod4(y + d))
    bias_send(1)

    own_bias.wait()

    for i in range(2):
        for k in range(2):
            n = (i * 2 + co) * 2 + k
            wait(kv.at[n], kv_recv.at[n])
            remote(kv.at[n], kv.at[n], kr_send.at[i * 2 + k], kv_recv.at[n], twin, b).start()

    for g in range(GROUPS):
        for j in (1, 3, 2):
            n = piece(z, mod4(y + j), 0)
            landed(g, n)
            for d in (1, 3, 2):
                spread(g, n, 5 + 3 * j + d, mod4(z + d), y)
            n = piece(mod4(z + j), y, 1)
            landed(g, n)
            for d in (3, 1, 2):
                spread(g, n, 17 + 3 * j + d, z, mod4(y + d))

    for i in range(2):
        for k in range(2):
            n = (i * 2 + 1 - co) * 2 + k
            wait(kv.at[n], kv_recv.at[n])

    def split(i):
        s, k, w = i // 4, (i // 2) % 2, i % 2
        rows = kv[s * 2 + k, w].astype(F32).T.astype(BF16)
        for h in range(NH):
            heads[w, s, h, block(k, KEYS), :] = rows[:, h * HD:(h + 1) * HD]
    loop(16, split)

    def rows_of(s, w, g, hh, y0):
        return jnp.concatenate([qa[piece(s, y0, xs), g, w, block(hh, HD), :] for xs in range(2)], axis=1)

    def stats_group(g, between):
        for i in ORDER:
            y0 = mod4(y + i)
            cols = block(y0, CH)
            if i > 0:
                for d in (1, 2, 3):
                    landed(g, piece(mod4(z + d), y0, 0))
                for d in range(4):
                    landed(g, piece(mod4(z + d), y0, 1))
            else:
                for d in (1, 2, 3):
                    landed(g, piece(mod4(z + d), y0, 0))
            for xs in range(2):
                bias_piece(g, xs * 4 + y0).wait_recv()

            def stats(hh):
                h = g * GH + hh
                add = jnp.concatenate([
                    jnp.concatenate([dot(eye[...], bias_in[k, h, block(xs * 4 + y0, BLK), :], NT) for xs in range(2)], axis=1)
                    for k in range(2)], axis=0)
                for s in range(SEQS):
                    sc = dot(heads[0, s, h], rows_of(s, 0, g, hh, y0), NN) + add
                    top = jnp.max(sc, axis=0, keepdims=True)
                    e = jnp.exp(sc - top)
                    pg = dot(heads[1, s, h], rows_of(s, 1, g, hh, y0), NN)
                    n = s * 4 + y0
                    stat[g, n, pl.ds(hh, 1), :] = top
                    stat[g, n, pl.ds(2 + hh, 1), :] = jnp.sum(e, axis=0, keepdims=True)
                    stat[g, n, pl.ds(4 + hh, 1), :] = jnp.sum(e * pg, axis=0, keepdims=True)
                    kept[s, h, :, cols] = e
                    kept_pg[s, h, :, cols] = pg
            loop(GH, stats)

            for s in range(SEQS):
                n = s * 4 + y0
                push(stat.at[g, n], stat_in.at[g, z * 4 + y], st_send.at[g * 16 + n],
                     st_recv.at[g * 16 + z * 4 + y], a, at(s, xl, y0))
            if i == 1:
                between()

    def combine(g):
        for i in range(16):
            wait(stat_in.at[g, i], st_recv.at[g * 16 + i])
        top = stat_in[g, 0, 0:2, :]
        for i in range(1, 16):
            top = jnp.maximum(top, stat_in[g, i, 0:2, :])
        el = jnp.zeros((2, CH), F32)
        ed = jnp.zeros((2, CH), F32)
        for i in range(16):
            fix = jnp.exp(stat_in[g, i, 0:2, :] - top)
            el = el + stat_in[g, i, 2:4, :] * fix
            ed = ed + stat_in[g, i, 4:6, :] * fix
        norm[g, 0:2, :] = top + jnp.log(el)
        norm[g, 2:4, :] = ed / el
        for i in BACK:
            for j in range(4):
                zz, yy = mod4(z + j), mod4(y + 4 - i)
                push(norm.at[g], norm_in.at[g, z * 4 + y], nm_send.at[g * 16 + zz * 4 + yy],
                     nm_recv.at[g * 16 + z * 4 + y], a, at(zz, xl, yy))

    def db_own(g, n):
        rows = block(n, BLK)
        return pltpu.make_async_copy(
            db_t.at[xl, pl.ds(g * GH, GH), rows, :], db_hbm.at[pl.ds(xl * NH + g * GH, GH), rows, :], dl_sem.at[g * 8 + n])

    def db_far(g, n):
        rows = block(n, BLK)
        return remote(
            db_t.at[px, pl.ds(g * GH, GH), rows, :], db_hbm.at[pl.ds(xl * NH + g * GH, GH), rows, :],
            ds_sem.at[g * 8 + n], dr_sem.at[g * 8 + n], a, at(z, px, y))

    def grads_group(g):
        for i in BACK:
            y0 = mod4(y + i)
            cols = block(y0, CH)
            for s in range(SEQS):
                n = s * 4 + y0
                wait(norm_in.at[g, n], nm_recv.at[g * 16 + n])

            def grads(hh):
                h = g * GH + hh
                hr = block(h, HD)
                gr = block(hh, HD)
                acc = None
                for s in range(SEQS):
                    n = s * 4 + y0
                    qh = rows_of(s, 0, g, hh, y0)
                    gh = rows_of(s, 1, g, hh, y0)
                    fix = jnp.exp(stat[g, n, pl.ds(hh, 1), :] - norm_in[g, n, pl.ds(hh, 1), :])
                    p = kept[s, h, :, cols] * fix
                    ds = p * (kept_pg[s, h, :, cols] - norm_in[g, n, pl.ds(2 + hh, 1), :])
                    acc = ds if acc is None else acc + ds
                    pb = p.astype(BF16)
                    sb = ds.astype(BF16)
                    kh = jnp.concatenate([kv[s * 2 + k, 0, hr, :] for k in range(2)], axis=1)
                    vh = jnp.concatenate([kv[s * 2 + k, 1, hr, :] for k in range(2)], axis=1)
                    part_o[g, s, y0, gr, :] = dot(vh, pb, NN).astype(BF16)
                    part_q[y0, g, s, gr, :] = dot(kh, sb, NN).astype(BF16)
                    dkv[s, 0, h] += dot(sb, qh, NT)
                    dkv[s, 1, h] += dot(pb, gh, NT)
                for k in range(2):
                    for xs in range(2):
                        tile = acc[k * KEYS:(k + 1) * KEYS, xs * BLK:(xs + 1) * BLK]
                        db_t[k, h, block(xs * 4 + y0, BLK), :] = tile.T.astype(BF16)
            loop(GH, grads)

            for xs in range(2):
                db_far(g, xs * 4 + y0).start()
                db_own(g, xs * 4 + y0).start()
            for d in (2, 1, 3):
                zz = mod4(z + d)
                remote(part_o.at[g, zz, y0], in_o.at[g, d, y0], o1_send.at[g * 16 + d * 4 + i],
                       o1_recv.at[g * 16 + d * 4 + y0], a, at(zz, xl, y)).start()
            if i > 0:
                remote(part_q.at[y0, g], in_q.at[i, g], q1_send.at[g * 4 + i], q1_recv.at[g * 4 + i], a, at(z, xl, y0)).start()

        for s in range(SEQS):
            for k in range(2):
                tiles = [dkv[s, w, g * GH + hh, k * KEYS:(k + 1) * KEYS, :] for w in range(2) for hh in range(GH)]
                dkv_out[g, s * 2 + k] = jnp.concatenate(tiles, axis=1).astype(BF16)
        for i in range(2):
            for k in range(2):
                remote(dkv_out.at[g, (i * 2 + 1 - co) * 2 + k], dkv_mid.at[g, i * 2 + k],
                       dm_send.at[g * 4 + i * 2 + k], dm_recv.at[g * 4 + i * 2 + k], twin, b).start()

    def key_grads(g):
        for j in range(2):
            i = lax.rem(xh + 1 + j, 2)
            for k in range(2):
                n = i * 2 + k
                wait(dkv_mid.at[g, n], dm_recv.at[g * 4 + n])
                both = dkv_out[g, (i * 2 + co) * 2 + k].astype(F32) + dkv_mid[g, n].astype(F32)
                dkv_sum[g, n] = both.astype(BF16)
                push(dkv_sum.at[g, n], dkv_in.at[g, xh * 2 + xl], dk_send.at[g * 4 + n],
                     dk_recv.at[g * 4 + xh * 2 + xl], i * 2 + co, at(z, k, y))

    dkv[...] = jnp.zeros_like(dkv)
    stats_group(0, lambda: None)
    stats_group(1, lambda: combine(0))
    grads_group(0)
    combine(1)
    key_grads(0)
    grads_group(1)
    key_grads(1)

    for g in range(GROUPS):
        for d in (1, 2, 3):
            wait(in_q.at[d, g], q1_recv.at[g * 4 + d])
    for i in BACK:
        zz = mod4(z + i)
        accs = []
        for g in range(GROUPS):
            acc = part_q[y, g, zz].astype(F32)
            for d in (1, 2, 3):
                acc = acc + in_q[d, g, zz].astype(F32)
            accs.append(acc)
        acc = jnp.concatenate(accs, axis=0)
        if i > 0:
            mid_q[i] = acc.astype(BF16)
            remote(mid_q.at[i], mid_q_in.at[i], q2_send.at[i], q2_recv.at[i], a, at(zz, xl, y)).start()
        else:
            sum_q = acc
    for i in BACK:
        yy = mod4(y + i)
        accs = []
        for g in range(GROUPS):
            acc = part_o[g, z, yy].astype(F32)
            for d in (1, 2, 3):
                wait(in_o.at[g, d, yy], o1_recv.at[g * 16 + d * 4 + yy])
                acc = acc + in_o[g, d, yy].astype(F32)
            accs.append(acc)
        acc = jnp.concatenate(accs, axis=0)
        if i > 0:
            mid_o[i] = acc.astype(BF16)
            remote(mid_o.at[i], mid_o_in.at[i], o2_send.at[i], o2_recv.at[i], a, at(z, xl, yy)).start()
        else:
            sum_o = acc
    for d in (1, 3, 2):
        wait(mid_q_in.at[d], q2_recv.at[d])
        sum_q = sum_q + mid_q_in[d].astype(F32)
    for d in (1, 3, 2):
        wait(mid_o_in.at[d], o2_recv.at[d])
        sum_o = sum_o + mid_o_in[d].astype(F32)
    for xs in range(2):
        cut = slice(xs * BLK, (xs + 1) * BLK)
        fin_out[xs, 0] = sum_o[:, cut].astype(BF16)
        fin_out[xs, 1] = sum_q[:, cut].astype(BF16)
        push(fin_out.at[xs], fin.at[xl], fin_send.at[xs], fin_recv.at[xl], z, at(a, xs, y))

    hom = jnp.zeros((BLK, WIDTH), F32)
    for g in range(GROUPS):
        for i in range(4):
            wait(dkv_in.at[g, i], dk_recv.at[g * 4 + i])
        for h in range(2):
            acc = (dkv_in[g, h].astype(F32) + dkv_in[g, 2 + h].astype(F32)).astype(BF16)
            cut = slice(h * HALF + g * GW, h * HALF + (g + 1) * GW)
            hom = hom + dot(acc[:, :GW], wk_ref[:, cut], NT) + dot(acc[:, GW:], wv_ref[:, cut], NT)
    for h in range(2):
        wait(fin.at[h], fin_recv.at[h])
        cut = slice(h * HALF, (h + 1) * HALF)
        og = gate[cut, :]
        dl = (gated[cut, :] * fin[h, 0].astype(F32) * og * (1.0 - og)).astype(BF16)
        dq = (fin[h, 1].astype(F32) * SCALE).astype(BF16)
        hom = hom + dot(dq, wq_ref[:, cut], TT) + dot(dl, wg_ref[:, cut], TT)
    hom_ref[...] = hom.astype(BF16)

    for h in range(2):
        pushed(fin_out.at[h], fin_send.at[h], z, at(a, h, y))
        for s in range(2):
            pushed(kvm.at[h], kv_send.at[s * 2 + h], s * 2 + co, at(z, h, y))
            wait(kv.at[0], kr_send.at[s * 2 + h])
    for g in range(GROUPS):
        for h in range(2):
            pushed(mine.at[h, g], s0_send.at[g * 2 + h], z, at(a, h, y))
            for s in range(2):
                n = s * 2 + h
                wait(dkv_mid.at[g, n], dm_send.at[g * 4 + n])
                pushed(dkv_sum.at[g, n], dk_send.at[g * 4 + n], s * 2 + co, at(z, h, y))
        for k in range(30):
            wait(qa.at[0, g], qa_send.at[g * 30 + k])
        for n in range(16):
            pushed(stat.at[g, n], st_send.at[g * 16 + n], a, at(n // 4, xl, n % 4))
            pushed(norm.at[g], nm_send.at[g * 16 + n], a, at(n // 4, xl, n % 4))
        for d in (1, 2, 3):
            for i in range(4):
                wait(part_o.at[g, 0, 0], o1_send.at[g * 16 + d * 4 + i])
            wait(part_q.at[0, g], q1_send.at[g * 4 + d])
        for n in range(8):
            bias_piece(g, n).wait_send()
            db_own(g, n).wait()
            db_far(g, n).wait()
    for d in (1, 2, 3):
        wait(mid_o.at[d], o2_send.at[d])
        wait(mid_q.at[d], q2_send.at[d])


def on_device(x, g, wq, wk, wv, wg, wr, bias):
    vm = pl.BlockSpec(memory_space=pltpu.VMEM)
    hbm = pl.BlockSpec(memory_space=pl.ANY)
    dma = pltpu.SemaphoreType.DMA
    V = pltpu.VMEM
    hom, db = pl.pallas_call(
        kernel,
        out_shape=[
            jax.ShapeDtypeStruct((BLK, WIDTH), BF16),
            jax.ShapeDtypeStruct((HEADS, ROWS, KEYS), BF16),
        ],
        in_specs=[vm] * 7 + [hbm],
        out_specs=[vm, hbm],
        scratch_shapes=[
            V((2, NH, ROWS, KEYS), BF16),
            V((KEYS, KEYS), BF16),
            V((2, GROUPS, 2, GW, BLK), BF16),
            V((2, 2, HALF, BLK), BF16),
            V((32, GROUPS, 2, GW, BLK), BF16),
            V((8, 2, HALF, KEYS), BF16),
            V((2, SEQS, NH, 2 * KEYS, HD), BF16),
            V((WIDTH, BLK), F32),
            V((WIDTH, BLK), F32),
            V((SEQS, NH, 2 * KEYS, ROWS), F32),
            V((SEQS, NH, 2 * KEYS, ROWS), F32),
            V((GROUPS, 16, 8, CH), F32),
            V((GROUPS, 16, 8, CH), F32),
            V((GROUPS, 8, CH), F32),
            V((GROUPS, 16, 8, CH), F32),
            V((GROUPS, 4, 4, GW, CH), BF16),
            V((4, GROUPS, 4, GW, CH), BF16),
            V((GROUPS, 4, 4, GW, CH), BF16),
            V((4, GROUPS, 4, GW, CH), BF16),
            V((4, HALF, CH), BF16),
            V((4, HALF, CH), BF16),
            V((4, HALF, CH), BF16),
            V((4, HALF, CH), BF16),
            V((2, 2, HALF, BLK), BF16),
            V((2, 2, HALF, BLK), BF16),
            V((SEQS, 2, NH, 2 * KEYS, HD), F32),
            V((GROUPS, 8, KEYS, HALF), BF16),
            V((GROUPS, 4, KEYS, HALF), BF16),
            V((GROUPS, 4, KEYS, HALF), BF16),
            V((GROUPS, 4, KEYS, HALF), BF16),
            V((2, NH, ROWS, KEYS), BF16),
            dma(()), dma((16,)), dma((16,)),
            dma((4,)), dma((60,)), dma((64,)),
            dma((4,)), dma((8,)), dma((4,)),
            dma((32,)), dma((32,)),
            dma((32,)), dma((32,)),
            dma((32,)), dma((32,)),
            dma((8,)), dma((8,)),
            dma((4,)), dma((4,)),
            dma((4,)), dma((4,)),
            dma((2,)), dma((2,)),
            dma((8,)), dma((8,)),
            dma((8,)), dma((8,)),
            dma((16,)), dma((16,)), dma((16,)),
        ],
        compiler_params=pltpu.CompilerParams(
            vmem_limit_bytes=60 * 2 ** 20, has_side_effects=True, collective_id=0),
        cost_estimate=pl.CostEstimate(flops=3 * 10 ** 9, bytes_accessed=10 ** 7, transcendentals=8 * 10 ** 6),
    )(x[0], g[0], wq, wk, wv, wg, wr, bias)
    return hom[None], db.astype(F32)


def solution(mesh):
    return jax.shard_map(
        on_device,
        mesh=mesh,
        in_specs=(
            P("seq", "res", None), P("seq", "res", None), P(), P(), P(), P(), P(),
            P(None, "seq", "res"),
        ),
        out_specs=(P("seq", "res", None), P(None, "seq", "res")),
        check_vma=False,
    )
```

```python
import jax
import jax.numpy as jnp
from jax import lax
from jax.experimental import pallas as pl
from jax.experimental.pallas import tpu as pltpu
from jax.sharding import PartitionSpec as P

HEADS = 8
NH = 4
GROUPS = 2
GH = 2
GW = 64
HD = 32
WIDTH = 256
HALF = 128
ROWS = 1024
KEYS = 128
SEQS = 4
BLK = 128
CH = 256
F32 = jnp.float32
BF16 = jnp.bfloat16
MESH = pl.DeviceIdType.MESH
SCALE = HD ** -0.5
ORDER = (0, 1, 3, 2)
BACK = (2, 3, 1, 0)

NN = ((1,), (0,))
NT = ((1,), (1,))
TT = ((0,), (1,))


def dot(a, b, dims):
    return lax.dot_general(a, b, (dims, ((), ())), preferred_element_type=F32)


def loop(n, body):
    def step(i, carry):
        body(i)
        return carry
    lax.fori_loop(0, n, step, 0)


def block(i, n):
    return pl.ds(pl.multiple_of(i * n, n), n)


def mod4(v):
    return lax.rem(v, 4)


def kernel(
    x_ref, g_ref, wq_ref, wk_ref, wv_ref, wg_ref, wr_ref, bias_hbm,
    hom_ref, db_hbm,
    bias_in, eye, mine, kvm, qa, kv, heads, gate, gated, kept, kept_pg,
    stat, stat_in, norm, norm_in, part_o, part_q, in_o, in_q, mid_o, mid_q, mid_o_in, mid_q_in,
    fin_out, fin, dkv, dkv_out, dkv_mid, dkv_sum, dkv_in, db_t,
    bl_sem, bs_sem, br_sem, s0_send, qa_send, qa_recv, kv_send, kv_recv, kr_send, st_send, st_recv, nm_send, nm_recv,
    o1_send, o1_recv, q1_send, q1_recv, o2_send, o2_recv, q2_send, q2_recv, fin_send, fin_recv,
    dm_send, dm_recv, dk_send, dk_recv, dl_sem, ds_sem, dr_sem,
):
    a = lax.axis_index("seq")
    b = lax.axis_index("res")
    z, xl, y = b // 8, (b // 4) % 2, b % 4
    px = 1 - xl
    xh, co = a // 2, a % 2
    twin = a + 1 - 2 * co

    def at(zz, xx, yy):
        return zz * 8 + xx * 4 + yy

    def remote(src, dst, send, recv, seq, res):
        return pltpu.make_async_remote_copy(
            src_ref=src, dst_ref=dst, send_sem=send, recv_sem=recv,
            device_id=(seq, res), device_id_type=MESH)

    def push(src, dst, send, recv, seq, res):
        here = jnp.logical_and(seq == a, res == b)

        @pl.when(here)
        def _():
            pltpu.make_async_copy(src, dst, recv).start()

        @pl.when(jnp.logical_not(here))
        def _():
            remote(src, dst, send, recv, seq, res).start()

    def pushed(src, send, seq, res):
        here = jnp.logical_and(seq == a, res == b)

        @pl.when(jnp.logical_not(here))
        def _():
            pltpu.make_async_copy(src, src, send).wait()

    def wait(ref, sem):
        pltpu.make_async_copy(ref, ref, sem).wait()

    barrier = pltpu.get_barrier_semaphore()

    def greet(seq, res):
        @pl.when(jnp.logical_not(jnp.logical_and(seq == a, res == b)))
        def _():
            pl.semaphore_signal(barrier, inc=1, device_id=(seq, res), device_id_type=MESH)

    for h in range(2):
        greet(z, at(a, h, y))
        for s in range(2):
            greet(s * 2 + co, at(z, h, y))
    greet(twin, b)
    for zz in range(4):
        for yy in range(4):
            greet(a, at(zz, xl, yy))

    own_bias = pltpu.make_async_copy(bias_hbm.at[pl.ds(xl * NH, NH)], bias_in.at[xl], bl_sem)
    own_bias.start()

    same = lax.broadcasted_iota(jnp.int32, (KEYS, KEYS), 0) == lax.broadcasted_iota(jnp.int32, (KEYS, KEYS), 1)
    eye[...] = jnp.where(same, 1.0, 0.0).astype(BF16)

    x = x_ref[...]
    qt = (dot(wq_ref[...], x, TT) * SCALE).astype(BF16)
    open_gate = jax.nn.sigmoid(dot(wg_ref[...], x, TT))
    gg = dot(wr_ref[...], g_ref[...], NT)
    gt = (gg * open_gate).astype(BF16)
    gate[...] = open_gate
    gated[...] = gg
    kt = dot(wk_ref[...], x, TT).astype(BF16)
    vt = dot(wv_ref[...], x, TT).astype(BF16)
    for h in range(2):
        for g in range(GROUPS):
            cut = slice(h * HALF + g * GW, h * HALF + (g + 1) * GW)
            mine[h, g, 0] = qt[cut]
            mine[h, g, 1] = gt[cut]
        cut = slice(h * HALF, (h + 1) * HALF)
        kvm[h, 0] = kt[cut]
        kvm[h, 1] = vt[cut]

    dkv[...] = jnp.zeros_like(dkv)
    pl.semaphore_wait(barrier, jnp.where(a == z, 20, 21))

    slot = (a * 4 + y) * 2 + xl
    for g in range(GROUPS):
        for h in range(2):
            push(mine.at[h, g], qa.at[slot, g], s0_send.at[g * 2 + h], qa_recv.at[g * 32 + slot], z, at(a, h, y))
    for i in range(2):
        s = lax.rem(xh + i, 2)
        for h in range(2):
            push(kvm.at[h], kv.at[a * 2 + xl], kv_send.at[s * 2 + h], kv_recv.at[a * 2 + xl], s * 2 + co, at(z, h, y))

    def bias_piece(g, n):
        rows = block(n, BLK)
        return remote(
            bias_hbm.at[pl.ds(px * NH + g * GH, GH), rows, :], bias_in.at[xl, pl.ds(g * GH, GH), rows, :],
            bs_sem.at[g * 8 + n], br_sem.at[g * 8 + n], a, at(z, px, y))

    def bias_send(g):
        for i in ORDER:
            for xs in range(2):
                bias_piece(g, xs * 4 + mod4(y + i)).start()

    def piece(z0, y0, xs):
        return (z0 * 4 + y0) * 2 + xs

    def landed(g, n):
        wait(qa.at[n, g], qa_recv.at[g * 32 + n])

    def spread(g, n, k, zz, yy):
        remote(qa.at[n, g], qa.at[n, g], qa_send.at[g * 30 + k], qa_recv.at[g * 32 + n], a, at(zz, xl, yy)).start()

    bias_send(0)
    home = [piece(z, y, 0), piece(z, y, 1)]
    for g in range(GROUPS):
        landed(g, home[0])
        for d in (3, 1, 2):
            spread(g, home[0], d - 1, z, mod4(y + d))
        landed(g, home[1])
        for d in (3, 1, 2):
            spread(g, home[1], 2 + d, mod4(z + d), y)
        for d in (1, 3, 2):
            spread(g, home[0], 5 + d, mod4(z + d), y)
        for d in (3, 1, 2):
            spread(g, home[1], 17 + d, z, mod4(y + d))
    bias_send(1)

    own_bias.wait()

    for i in range(2):
        for k in range(2):
            n = (i * 2 + co) * 2 + k
            wait(kv.at[n], kv_recv.at[n])
            remote(kv.at[n], kv.at[n], kr_send.at[i * 2 + k], kv_recv.at[n], twin, b).start()

    for g in range(GROUPS):
        for j in (1, 3, 2):
            n = piece(z, mod4(y + j), 0)
            landed(g, n)
            for d in (1, 3, 2):
                spread(g, n, 5 + 3 * j + d, mod4(z + d), y)
            n = piece(mod4(z + j), y, 1)
            landed(g, n)
            for d in (3, 1, 2):
                spread(g, n, 17 + 3 * j + d, z, mod4(y + d))

    for i in range(2):
        for k in range(2):
            n = (i * 2 + 1 - co) * 2 + k
            wait(kv.at[n], kv_recv.at[n])

    def split(i):
        s, k, w = i // 4, (i // 2) % 2, i % 2
        rows = kv[s * 2 + k, w].astype(F32).T.astype(BF16)
        for h in range(NH):
            heads[w, s, h, block(k, KEYS), :] = rows[:, h * HD:(h + 1) * HD]
    loop(16, split)

    def rows_of(s, w, g, hh, y0):
        return jnp.concatenate([qa[piece(s, y0, xs), g, w, block(hh, HD), :] for xs in range(2)], axis=1)

    def stats_group(g, between):
        for i in ORDER:
            y0 = mod4(y + i)
            cols = block(y0, CH)
            if i > 0:
                for d in (1, 2, 3):
                    landed(g, piece(mod4(z + d), y0, 0))
                for d in range(4):
                    landed(g, piece(mod4(z + d), y0, 1))
            else:
                for d in (1, 2, 3):
                    landed(g, piece(mod4(z + d), y0, 0))
            for xs in range(2):
                bias_piece(g, xs * 4 + y0).wait_recv()

            def stats(hh):
                h = g * GH + hh
                add = jnp.concatenate([
                    jnp.concatenate([dot(eye[...], bias_in[k, h, block(xs * 4 + y0, BLK), :], NT) for xs in range(2)], axis=1)
                    for k in range(2)], axis=0)
                for s in range(SEQS):
                    sc = dot(heads[0, s, h], rows_of(s, 0, g, hh, y0), NN) + add
                    top = jnp.max(sc, axis=0, keepdims=True)
                    e = jnp.exp(sc - top)
                    pg = dot(heads[1, s, h], rows_of(s, 1, g, hh, y0), NN)
                    n = s * 4 + y0
                    stat[g, n, pl.ds(hh, 1), :] = top
                    stat[g, n, pl.ds(2 + hh, 1), :] = jnp.sum(e, axis=0, keepdims=True)
                    stat[g, n, pl.ds(4 + hh, 1), :] = jnp.sum(e * pg, axis=0, keepdims=True)
                    kept[s, h, :, cols] = e
                    kept_pg[s, h, :, cols] = pg
            for hh in range(GH):
                stats(hh)

            for s in range(SEQS):
                n = s * 4 + y0
                push(stat.at[g, n], stat_in.at[g, z * 4 + y], st_send.at[g * 16 + n],
                     st_recv.at[g * 16 + z * 4 + y], a, at(s, xl, y0))
            if i == 1:
                between()

    def combine(g):
        for i in range(16):
            wait(stat_in.at[g, i], st_recv.at[g * 16 + i])
        top = stat_in[g, 0, 0:2, :]
        for i in range(1, 16):
            top = jnp.maximum(top, stat_in[g, i, 0:2, :])
        el = jnp.zeros((2, CH), F32)
        ed = jnp.zeros((2, CH), F32)
        for i in range(16):
            fix = jnp.exp(stat_in[g, i, 0:2, :] - top)
            el = el + stat_in[g, i, 2:4, :] * fix
            ed = ed + stat_in[g, i, 4:6, :] * fix
        norm[g, 0:2, :] = top + jnp.log(el)
        norm[g, 2:4, :] = ed / el
        for i in BACK:
            for j in range(4):
                zz, yy = mod4(z + j), mod4(y + 4 - i)
                push(norm.at[g], norm_in.at[g, z * 4 + y], nm_send.at[g * 16 + zz * 4 + yy],
                     nm_recv.at[g * 16 + z * 4 + y], a, at(zz, xl, yy))

    def db_own(g, n):
        rows = block(n, BLK)
        return pltpu.make_async_copy(
            db_t.at[xl, pl.ds(g * GH, GH), rows, :], db_hbm.at[pl.ds(xl * NH + g * GH, GH), rows, :], dl_sem.at[g * 8 + n])

    def db_far(g, n):
        rows = block(n, BLK)
        return remote(
            db_t.at[px, pl.ds(g * GH, GH), rows, :], db_hbm.at[pl.ds(xl * NH + g * GH, GH), rows, :],
            ds_sem.at[g * 8 + n], dr_sem.at[g * 8 + n], a, at(z, px, y))

    def grads_group(g):
        for i in BACK:
            y0 = mod4(y + i)
            cols = block(y0, CH)
            for s in range(SEQS):
                n = s * 4 + y0
                wait(norm_in.at[g, n], nm_recv.at[g * 16 + n])

            def grads(hh):
                h = g * GH + hh
                hr = block(h, HD)
                gr = block(hh, HD)
                acc = None
                for s in range(SEQS):
                    n = s * 4 + y0
                    qh = rows_of(s, 0, g, hh, y0)
                    gh = rows_of(s, 1, g, hh, y0)
                    fix = jnp.exp(stat[g, n, pl.ds(hh, 1), :] - norm_in[g, n, pl.ds(hh, 1), :])
                    p = kept[s, h, :, cols] * fix
                    ds = p * (kept_pg[s, h, :, cols] - norm_in[g, n, pl.ds(2 + hh, 1), :])
                    acc = ds if acc is None else acc + ds
                    pb = p.astype(BF16)
                    sb = ds.astype(BF16)
                    kh = jnp.concatenate([kv[s * 2 + k, 0, hr, :] for k in range(2)], axis=1)
                    vh = jnp.concatenate([kv[s * 2 + k, 1, hr, :] for k in range(2)], axis=1)
                    part_o[g, s, y0, gr, :] = dot(vh, pb, NN).astype(BF16)
                    part_q[y0, g, s, gr, :] = dot(kh, sb, NN).astype(BF16)
                    dkv[s, 0, h] += dot(sb, qh, NT)
                    dkv[s, 1, h] += dot(pb, gh, NT)
                for k in range(2):
                    for xs in range(2):
                        tile = acc[k * KEYS:(k + 1) * KEYS, xs * BLK:(xs + 1) * BLK]
                        db_t[k, h, block(xs * 4 + y0, BLK), :] = tile.T.astype(BF16)
            for hh in range(GH):
                grads(hh)

            for xs in range(2):
                db_far(g, xs * 4 + y0).start()
                db_own(g, xs * 4 + y0).start()
            for d in (2, 1, 3):
                zz = mod4(z + d)
                remote(part_o.at[g, zz, y0], in_o.at[g, d, y0], o1_send.at[g * 16 + d * 4 + i],
                       o1_recv.at[g * 16 + d * 4 + y0], a, at(zz, xl, y)).start()
            if i > 0:
                remote(part_q.at[y0, g], in_q.at[i, g], q1_send.at[g * 4 + i], q1_recv.at[g * 4 + i], a, at(z, xl, y0)).start()

        for s in range(SEQS):
            for k in range(2):
                tiles = [dkv[s, w, g * GH + hh, k * KEYS:(k + 1) * KEYS, :] for w in range(2) for hh in range(GH)]
                dkv_out[g, s * 2 + k] = jnp.concatenate(tiles, axis=1).astype(BF16)
        for i in range(2):
            for k in range(2):
                remote(dkv_out.at[g, (i * 2 + 1 - co) * 2 + k], dkv_mid.at[g, i * 2 + k],
                       dm_send.at[g * 4 + i * 2 + k], dm_recv.at[g * 4 + i * 2 + k], twin, b).start()

    def key_grads(g):
        for j in range(2):
            i = lax.rem(xh + 1 + j, 2)
            for k in range(2):
                n = i * 2 + k
                wait(dkv_mid.at[g, n], dm_recv.at[g * 4 + n])
                both = dkv_out[g, (i * 2 + co) * 2 + k].astype(F32) + dkv_mid[g, n].astype(F32)
                dkv_sum[g, n] = both.astype(BF16)
                push(dkv_sum.at[g, n], dkv_in.at[g, xh * 2 + xl], dk_send.at[g * 4 + n],
                     dk_recv.at[g * 4 + xh * 2 + xl], i * 2 + co, at(z, k, y))

    stats_group(0, lambda: None)
    stats_group(1, lambda: combine(0))
    grads_group(0)
    combine(1)
    key_grads(0)
    grads_group(1)
    key_grads(1)

    for g in range(GROUPS):
        for d in (1, 2, 3):
            wait(in_q.at[d, g], q1_recv.at[g * 4 + d])
    for i in BACK:
        zz = mod4(z + i)
        accs = []
        for g in range(GROUPS):
            acc = part_q[y, g, zz].astype(F32)
            for d in (1, 2, 3):
                acc = acc + in_q[d, g, zz].astype(F32)
            accs.append(acc)
        acc = jnp.concatenate(accs, axis=0)
        if i > 0:
            mid_q[i] = acc.astype(BF16)
            remote(mid_q.at[i], mid_q_in.at[i], q2_send.at[i], q2_recv.at[i], a, at(zz, xl, y)).start()
        else:
            sum_q = acc
    for i in BACK:
        yy = mod4(y + i)
        accs = []
        for g in range(GROUPS):
            acc = part_o[g, z, yy].astype(F32)
            for d in (1, 2, 3):
                wait(in_o.at[g, d, yy], o1_recv.at[g * 16 + d * 4 + yy])
                acc = acc + in_o[g, d, yy].astype(F32)
            accs.append(acc)
        acc = jnp.concatenate(accs, axis=0)
        if i > 0:
            mid_o[i] = acc.astype(BF16)
            remote(mid_o.at[i], mid_o_in.at[i], o2_send.at[i], o2_recv.at[i], a, at(z, xl, yy)).start()
        else:
            sum_o = acc
    for h in range(2):
        for s in range(2):
            pushed(kvm.at[h], kv_send.at[s * 2 + h], s * 2 + co, at(z, h, y))
            wait(kv.at[0], kr_send.at[s * 2 + h])
    for g in range(GROUPS):
        for h in range(2):
            pushed(mine.at[h, g], s0_send.at[g * 2 + h], z, at(a, h, y))
            for s in range(2):
                n = s * 2 + h
                wait(dkv_mid.at[g, n], dm_send.at[g * 4 + n])
        for k in range(30):
            wait(qa.at[0, g], qa_send.at[g * 30 + k])
        for n in range(16):
            pushed(stat.at[g, n], st_send.at[g * 16 + n], a, at(n // 4, xl, n % 4))
            pushed(norm.at[g], nm_send.at[g * 16 + n], a, at(n // 4, xl, n % 4))
        for d in (1, 2, 3):
            for i in range(4):
                wait(part_o.at[g, 0, 0], o1_send.at[g * 16 + d * 4 + i])
            wait(part_q.at[0, g], q1_send.at[g * 4 + d])
        for n in range(8):
            bias_piece(g, n).wait_send()
    for d in (1, 3, 2):
        wait(mid_q_in.at[d], q2_recv.at[d])
        sum_q = sum_q + mid_q_in[d].astype(F32)
    for d in (1, 3, 2):
        wait(mid_o_in.at[d], o2_recv.at[d])
        sum_o = sum_o + mid_o_in[d].astype(F32)
    for xs in range(2):
        cut = slice(xs * BLK, (xs + 1) * BLK)
        fin_out[xs, 0] = sum_o[:, cut].astype(BF16)
        fin_out[xs, 1] = sum_q[:, cut].astype(BF16)
        push(fin_out.at[xs], fin.at[xl], fin_send.at[xs], fin_recv.at[xl], z, at(a, xs, y))

    hom = jnp.zeros((BLK, WIDTH), F32)
    for g in range(GROUPS):
        for i in range(4):
            wait(dkv_in.at[g, i], dk_recv.at[g * 4 + i])
        for h in range(2):
            acc = (dkv_in[g, h].astype(F32) + dkv_in[g, 2 + h].astype(F32)).astype(BF16)
            cut = slice(h * HALF + g * GW, h * HALF + (g + 1) * GW)
            hom = hom + dot(acc[:, :GW], wk_ref[:, cut], NT) + dot(acc[:, GW:], wv_ref[:, cut], NT)
    for h in range(2):
        wait(fin.at[h], fin_recv.at[h])
        cut = slice(h * HALF, (h + 1) * HALF)
        og = gate[cut, :]
        dl = (gated[cut, :] * fin[h, 0].astype(F32) * og * (1.0 - og)).astype(BF16)
        dq = (fin[h, 1].astype(F32) * SCALE).astype(BF16)
        hom = hom + dot(dq, wq_ref[:, cut], TT) + dot(dl, wg_ref[:, cut], TT)
    hom_ref[...] = hom.astype(BF16)

    for h in range(2):
        pushed(fin_out.at[h], fin_send.at[h], z, at(a, h, y))
        for s in range(2):
            for g in range(GROUPS):
                n = s * 2 + h
                pushed(dkv_sum.at[g, n], dk_send.at[g * 4 + n], s * 2 + co, at(z, h, y))
    for g in range(GROUPS):
        for n in range(8):
            db_own(g, n).wait()
            db_far(g, n).wait()
    for d in (1, 2, 3):
        wait(mid_o.at[d], o2_send.at[d])
        wait(mid_q.at[d], q2_send.at[d])


def on_device(x, g, wq, wk, wv, wg, wr, bias):
    vm = pl.BlockSpec(memory_space=pltpu.VMEM)
    hbm = pl.BlockSpec(memory_space=pl.ANY)
    dma = pltpu.SemaphoreType.DMA
    V = pltpu.VMEM
    hom, db = pl.pallas_call(
        kernel,
        out_shape=[
            jax.ShapeDtypeStruct((BLK, WIDTH), BF16),
            jax.ShapeDtypeStruct((HEADS, ROWS, KEYS), BF16),
        ],
        in_specs=[vm] * 7 + [hbm],
        out_specs=[vm, hbm],
        scratch_shapes=[
            V((2, NH, ROWS, KEYS), BF16),
            V((KEYS, KEYS), BF16),
            V((2, GROUPS, 2, GW, BLK), BF16),
            V((2, 2, HALF, BLK), BF16),
            V((32, GROUPS, 2, GW, BLK), BF16),
            V((8, 2, HALF, KEYS), BF16),
            V((2, SEQS, NH, 2 * KEYS, HD), BF16),
            V((WIDTH, BLK), F32),
            V((WIDTH, BLK), F32),
            V((SEQS, NH, 2 * KEYS, ROWS), F32),
            V((SEQS, NH, 2 * KEYS, ROWS), F32),
            V((GROUPS, 16, 8, CH), F32),
            V((GROUPS, 16, 8, CH), F32),
            V((GROUPS, 8, CH), F32),
            V((GROUPS, 16, 8, CH), F32),
            V((GROUPS, 4, 4, GW, CH), BF16),
            V((4, GROUPS, 4, GW, CH), BF16),
            V((GROUPS, 4, 4, GW, CH), BF16),
            V((4, GROUPS, 4, GW, CH), BF16),
            V((4, HALF, CH), BF16),
            V((4, HALF, CH), BF16),
            V((4, HALF, CH), BF16),
            V((4, HALF, CH), BF16),
            V((2, 2, HALF, BLK), BF16),
            V((2, 2, HALF, BLK), BF16),
            V((SEQS, 2, NH, 2 * KEYS, HD), F32),
            V((GROUPS, 8, KEYS, HALF), BF16),
            V((GROUPS, 4, KEYS, HALF), BF16),
            V((GROUPS, 4, KEYS, HALF), BF16),
            V((GROUPS, 4, KEYS, HALF), BF16),
            V((2, NH, ROWS, KEYS), BF16),
            dma(()), dma((16,)), dma((16,)),
            dma((4,)), dma((60,)), dma((64,)),
            dma((4,)), dma((8,)), dma((4,)),
            dma((32,)), dma((32,)),
            dma((32,)), dma((32,)),
            dma((32,)), dma((32,)),
            dma((8,)), dma((8,)),
            dma((4,)), dma((4,)),
            dma((4,)), dma((4,)),
            dma((2,)), dma((2,)),
            dma((8,)), dma((8,)),
            dma((8,)), dma((8,)),
            dma((16,)), dma((16,)), dma((16,)),
        ],
        compiler_params=pltpu.CompilerParams(
            vmem_limit_bytes=60 * 2 ** 20, has_side_effects=True, collective_id=0),
        cost_estimate=pl.CostEstimate(flops=3 * 10 ** 9, bytes_accessed=10 ** 7, transcendentals=8 * 10 ** 6),
    )(x[0], g[0], wq, wk, wv, wg, wr, bias)
    return hom[None], db.astype(F32)


def solution(mesh):
    return jax.shard_map(
        on_device,
        mesh=mesh,
        in_specs=(
            P("seq", "res", None), P("seq", "res", None), P(), P(), P(), P(), P(),
            P(None, "seq", "res"),
        ),
        out_specs=(P("seq", "res", None), P(None, "seq", "res")),
        check_vma=False,
    )
```

```python
import jax
import jax.numpy as jnp
from jax import lax
from jax.experimental import pallas as pl
from jax.experimental.pallas import tpu as pltpu
from jax.sharding import PartitionSpec as P

HEADS = 8
NH = 4
GROUPS = 2
GH = 2
GW = 64
HD = 32
WIDTH = 256
HALF = 128
ROWS = 1024
KEYS = 128
SEQS = 4
BLK = 128
CH = 256
F32 = jnp.float32
BF16 = jnp.bfloat16
MESH = pl.DeviceIdType.MESH
SCALE = HD ** -0.5
ORDER = (0, 1, 3, 2)
BACK = (2, 3, 1, 0)

NN = ((1,), (0,))
NT = ((1,), (1,))
TT = ((0,), (1,))


def dot(a, b, dims):
    return lax.dot_general(a, b, (dims, ((), ())), preferred_element_type=F32)


def loop(n, body):
    def step(i, carry):
        body(i)
        return carry
    lax.fori_loop(0, n, step, 0)


def block(i, n):
    return pl.ds(pl.multiple_of(i * n, n), n)


def mod4(v):
    return lax.rem(v, 4)


def kernel(
    x_ref, g_ref, wq_ref, wk_ref, wv_ref, wg_ref, wr_ref, bias_hbm,
    hom_ref, db_hbm,
    bias_in, eye, mine, kvm, qa, kv, heads, gate, gated, kept, kept_pg,
    stat, stat_in, norm, norm_in, part_o, part_q, in_o, in_q, mid_o, mid_q, mid_o_in, mid_q_in,
    fin_out, fin, dkv, dkv_out, dkv_mid, dkv_sum, dkv_in, db_t,
    bl_sem, bs_sem, br_sem, s0_send, qa_send, qa_recv, kv_send, kv_recv, kr_send, st_send, st_recv, nm_send, nm_recv,
    o1_send, o1_recv, q1_send, q1_recv, o2_send, o2_recv, q2_send, q2_recv, fin_send, fin_recv,
    dm_send, dm_recv, dk_send, dk_recv, dl_sem, ds_sem, dr_sem,
):
    a = lax.axis_index("seq")
    b = lax.axis_index("res")
    z, xl, y = b // 8, (b // 4) % 2, b % 4
    px = 1 - xl
    xh, co = a // 2, a % 2
    twin = a + 1 - 2 * co

    def at(zz, xx, yy):
        return zz * 8 + xx * 4 + yy

    def remote(src, dst, send, recv, seq, res):
        return pltpu.make_async_remote_copy(
            src_ref=src, dst_ref=dst, send_sem=send, recv_sem=recv,
            device_id=(seq, res), device_id_type=MESH)

    def push(src, dst, send, recv, seq, res):
        here = jnp.logical_and(seq == a, res == b)

        @pl.when(here)
        def _():
            pltpu.make_async_copy(src, dst, recv).start()

        @pl.when(jnp.logical_not(here))
        def _():
            remote(src, dst, send, recv, seq, res).start()

    def pushed(src, send, seq, res):
        here = jnp.logical_and(seq == a, res == b)

        @pl.when(jnp.logical_not(here))
        def _():
            pltpu.make_async_copy(src, src, send).wait()

    def wait(ref, sem):
        pltpu.make_async_copy(ref, ref, sem).wait()

    barrier = pltpu.get_barrier_semaphore()

    def greet(seq, res):
        @pl.when(jnp.logical_not(jnp.logical_and(seq == a, res == b)))
        def _():
            pl.semaphore_signal(barrier, inc=1, device_id=(seq, res), device_id_type=MESH)

    for h in range(2):
        greet(z, at(a, h, y))
        for s in range(2):
            greet(s * 2 + co, at(z, h, y))
    greet(twin, b)
    for zz in range(4):
        for yy in range(4):
            greet(a, at(zz, xl, yy))

    own_bias = pltpu.make_async_copy(bias_hbm.at[pl.ds(xl * NH, NH)], bias_in.at[xl], bl_sem)
    own_bias.start()

    same = lax.broadcasted_iota(jnp.int32, (KEYS, KEYS), 0) == lax.broadcasted_iota(jnp.int32, (KEYS, KEYS), 1)
    eye[...] = jnp.where(same, 1.0, 0.0).astype(BF16)

    x = x_ref[...]
    qt = (dot(wq_ref[...], x, TT) * SCALE).astype(BF16)
    open_gate = jax.nn.sigmoid(dot(wg_ref[...], x, TT))
    gg = dot(wr_ref[...], g_ref[...], NT)
    gt = (gg * open_gate).astype(BF16)
    gate[...] = open_gate
    gated[...] = gg
    kt = dot(wk_ref[...], x, TT).astype(BF16)
    vt = dot(wv_ref[...], x, TT).astype(BF16)
    for h in range(2):
        for g in range(GROUPS):
            cut = slice(h * HALF + g * GW, h * HALF + (g + 1) * GW)
            mine[h, g, 0] = qt[cut]
            mine[h, g, 1] = gt[cut]
        cut = slice(h * HALF, (h + 1) * HALF)
        kvm[h, 0] = kt[cut]
        kvm[h, 1] = vt[cut]

    pl.semaphore_wait(barrier, jnp.where(a == z, 20, 21))

    slot = (a * 4 + y) * 2 + xl
    for g in range(GROUPS):
        for h in range(2):
            push(mine.at[h, g], qa.at[slot, g], s0_send.at[g * 2 + h], qa_recv.at[g * 32 + slot], z, at(a, h, y))
    for i in range(2):
        s = lax.rem(xh + i, 2)
        for h in range(2):
            push(kvm.at[h], kv.at[a * 2 + xl], kv_send.at[s * 2 + h], kv_recv.at[a * 2 + xl], s * 2 + co, at(z, h, y))

    def bias_piece(g, n):
        rows = block(n, BLK)
        return remote(
            bias_hbm.at[pl.ds(px * NH + g * GH, GH), rows, :], bias_in.at[xl, pl.ds(g * GH, GH), rows, :],
            bs_sem.at[g * 8 + n], br_sem.at[g * 8 + n], a, at(z, px, y))

    def bias_send(g):
        for i in ORDER:
            for xs in range(2):
                bias_piece(g, xs * 4 + mod4(y + i)).start()

    def piece(z0, y0, xs):
        return (z0 * 4 + y0) * 2 + xs

    def landed(g, n):
        wait(qa.at[n, g], qa_recv.at[g * 32 + n])

    def spread(g, n, k, zz, yy):
        remote(qa.at[n, g], qa.at[n, g], qa_send.at[g * 30 + k], qa_recv.at[g * 32 + n], a, at(zz, xl, yy)).start()

    bias_send(0)
    home = [piece(z, y, 0), piece(z, y, 1)]
    for g in range(GROUPS):
        landed(g, home[0])
        for d in (3, 1, 2):
            spread(g, home[0], d - 1, z, mod4(y + d))
        landed(g, home[1])
        for d in (3, 1, 2):
            spread(g, home[1], 2 + d, mod4(z + d), y)
        for d in (1, 3, 2):
            spread(g, home[0], 5 + d, mod4(z + d), y)
        for d in (3, 1, 2):
            spread(g, home[1], 17 + d, z, mod4(y + d))
    bias_send(1)

    own_bias.wait()

    for i in range(2):
        for k in range(2):
            n = (i * 2 + co) * 2 + k
            wait(kv.at[n], kv_recv.at[n])
            remote(kv.at[n], kv.at[n], kr_send.at[i * 2 + k], kv_recv.at[n], twin, b).start()

    for g in range(GROUPS):
        for j in (1, 3, 2):
            n = piece(z, mod4(y + j), 0)
            landed(g, n)
            for d in (1, 3, 2):
                spread(g, n, 5 + 3 * j + d, mod4(z + d), y)
            n = piece(mod4(z + j), y, 1)
            landed(g, n)
            for d in (3, 1, 2):
                spread(g, n, 17 + 3 * j + d, z, mod4(y + d))

    for i in range(2):
        for k in range(2):
            n = (i * 2 + 1 - co) * 2 + k
            wait(kv.at[n], kv_recv.at[n])

    def split(i):
        s, k, w = i // 4, (i // 2) % 2, i % 2
        rows = kv[s * 2 + k, w].astype(F32).T.astype(BF16)
        for h in range(NH):
            heads[w, s, h, block(k, KEYS), :] = rows[:, h * HD:(h + 1) * HD]
    loop(16, split)

    def rows_of(s, w, g, hh, y0):
        return jnp.concatenate([qa[piece(s, y0, xs), g, w, block(hh, HD), :] for xs in range(2)], axis=1)

    def stats_group(g, between):
        for i in ORDER:
            y0 = mod4(y + i)
            cols = block(y0, CH)
            if i > 0:
                for d in (1, 2, 3):
                    landed(g, piece(mod4(z + d), y0, 0))
                for d in range(4):
                    landed(g, piece(mod4(z + d), y0, 1))
            else:
                for d in (1, 2, 3):
                    landed(g, piece(mod4(z + d), y0, 0))
            for xs in range(2):
                bias_piece(g, xs * 4 + y0).wait_recv()

            def stats(hh):
                h = g * GH + hh
                add = jnp.concatenate([
                    jnp.concatenate([dot(eye[...], bias_in[k, h, block(xs * 4 + y0, BLK), :], NT) for xs in range(2)], axis=1)
                    for k in range(2)], axis=0)
                for s in range(SEQS):
                    sc = dot(heads[0, s, h], rows_of(s, 0, g, hh, y0), NN) + add
                    top = jnp.max(sc, axis=0, keepdims=True)
                    e = jnp.exp(sc - top)
                    pg = dot(heads[1, s, h], rows_of(s, 1, g, hh, y0), NN)
                    n = s * 4 + y0
                    stat[g, n, pl.ds(hh, 1), :] = top
                    stat[g, n, pl.ds(2 + hh, 1), :] = jnp.sum(e, axis=0, keepdims=True)
                    stat[g, n, pl.ds(4 + hh, 1), :] = jnp.sum(e * pg, axis=0, keepdims=True)
                    kept[s, h, :, cols] = e
                    kept_pg[s, h, :, cols] = pg
            for hh in range(GH):
                stats(hh)

            for s in range(SEQS):
                n = s * 4 + y0
                push(stat.at[g, n], stat_in.at[g, z * 4 + y], st_send.at[g * 16 + n],
                     st_recv.at[g * 16 + z * 4 + y], a, at(s, xl, y0))
            if i == 1:
                between()

    def combine(g):
        for i in range(16):
            wait(stat_in.at[g, i], st_recv.at[g * 16 + i])
        top = stat_in[g, 0, 0:2, :]
        for i in range(1, 16):
            top = jnp.maximum(top, stat_in[g, i, 0:2, :])
        el = jnp.zeros((2, CH), F32)
        ed = jnp.zeros((2, CH), F32)
        for i in range(16):
            fix = jnp.exp(stat_in[g, i, 0:2, :] - top)
            el = el + stat_in[g, i, 2:4, :] * fix
            ed = ed + stat_in[g, i, 4:6, :] * fix
        norm[g, 0:2, :] = top + jnp.log(el)
        norm[g, 2:4, :] = ed / el
        for i in BACK:
            for j in range(4):
                zz, yy = mod4(z + j), mod4(y + 4 - i)
                push(norm.at[g], norm_in.at[g, z * 4 + y], nm_send.at[g * 16 + zz * 4 + yy],
                     nm_recv.at[g * 16 + z * 4 + y], a, at(zz, xl, yy))

    def db_own(g, n):
        rows = block(n, BLK)
        return pltpu.make_async_copy(
            db_t.at[xl, pl.ds(g * GH, GH), rows, :], db_hbm.at[pl.ds(xl * NH + g * GH, GH), rows, :], dl_sem.at[g * 8 + n])

    def db_far(g, n):
        rows = block(n, BLK)
        return remote(
            db_t.at[px, pl.ds(g * GH, GH), rows, :], db_hbm.at[pl.ds(xl * NH + g * GH, GH), rows, :],
            ds_sem.at[g * 8 + n], dr_sem.at[g * 8 + n], a, at(z, px, y))

    def grads_group(g):
        for i in BACK:
            y0 = mod4(y + i)
            cols = block(y0, CH)
            for s in range(SEQS):
                n = s * 4 + y0
                wait(norm_in.at[g, n], nm_recv.at[g * 16 + n])

            def grads(hh):
                h = g * GH + hh
                hr = block(h, HD)
                gr = block(hh, HD)
                acc = None
                for s in range(SEQS):
                    n = s * 4 + y0
                    qh = rows_of(s, 0, g, hh, y0)
                    gh = rows_of(s, 1, g, hh, y0)
                    fix = jnp.exp(stat[g, n, pl.ds(hh, 1), :] - norm_in[g, n, pl.ds(hh, 1), :])
                    p = kept[s, h, :, cols] * fix
                    ds = p * (kept_pg[s, h, :, cols] - norm_in[g, n, pl.ds(2 + hh, 1), :])
                    acc = ds if acc is None else acc + ds
                    pb = p.astype(BF16)
                    sb = ds.astype(BF16)
                    kh = jnp.concatenate([kv[s * 2 + k, 0, hr, :] for k in range(2)], axis=1)
                    vh = jnp.concatenate([kv[s * 2 + k, 1, hr, :] for k in range(2)], axis=1)
                    part_o[g, s, y0, gr, :] = dot(vh, pb, NN).astype(BF16)
                    part_q[y0, g, s, gr, :] = dot(kh, sb, NN).astype(BF16)
                    dk = dot(sb, qh, NT)
                    dv = dot(pb, gh, NT)
                    dkv[s, 0, h] = dk if i == BACK[0] else dkv[s, 0, h] + dk
                    dkv[s, 1, h] = dv if i == BACK[0] else dkv[s, 1, h] + dv
                for k in range(2):
                    for xs in range(2):
                        tile = acc[k * KEYS:(k + 1) * KEYS, xs * BLK:(xs + 1) * BLK]
                        db_t[k, h, block(xs * 4 + y0, BLK), :] = tile.T.astype(BF16)
            for hh in range(GH):
                grads(hh)

            for xs in range(2):
                db_far(g, xs * 4 + y0).start()
                db_own(g, xs * 4 + y0).start()
            for d in (2, 1, 3):
                zz = mod4(z + d)
                remote(part_o.at[g, zz, y0], in_o.at[g, d, y0], o1_send.at[g * 16 + d * 4 + i],
                       o1_recv.at[g * 16 + d * 4 + y0], a, at(zz, xl, y)).start()
            if i > 0:
                remote(part_q.at[y0, g], in_q.at[i, g], q1_send.at[g * 4 + i], q1_recv.at[g * 4 + i], a, at(z, xl, y0)).start()

        for s in range(SEQS):
            for k in range(2):
                tiles = [dkv[s, w, g * GH + hh, k * KEYS:(k + 1) * KEYS, :] for w in range(2) for hh in range(GH)]
                dkv_out[g, s * 2 + k] = jnp.concatenate(tiles, axis=1).astype(BF16)
        for i in range(2):
            for k in range(2):
                remote(dkv_out.at[g, (i * 2 + 1 - co) * 2 + k], dkv_mid.at[g, i * 2 + k],
                       dm_send.at[g * 4 + i * 2 + k], dm_recv.at[g * 4 + i * 2 + k], twin, b).start()

    def key_grads(g):
        for j in range(2):
            i = lax.rem(xh + 1 + j, 2)
            for k in range(2):
                n = i * 2 + k
                wait(dkv_mid.at[g, n], dm_recv.at[g * 4 + n])
                both = dkv_out[g, (i * 2 + co) * 2 + k].astype(F32) + dkv_mid[g, n].astype(F32)
                dkv_sum[g, n] = both.astype(BF16)
                push(dkv_sum.at[g, n], dkv_in.at[g, xh * 2 + xl], dk_send.at[g * 4 + n],
                     dk_recv.at[g * 4 + xh * 2 + xl], i * 2 + co, at(z, k, y))

    stats_group(0, lambda: None)
    stats_group(1, lambda: combine(0))
    grads_group(0)
    combine(1)
    key_grads(0)
    grads_group(1)
    key_grads(1)

    for g in range(GROUPS):
        for d in (1, 2, 3):
            wait(in_q.at[d, g], q1_recv.at[g * 4 + d])
    for i in BACK:
        zz = mod4(z + i)
        accs = []
        for g in range(GROUPS):
            acc = part_q[y, g, zz].astype(F32)
            for d in (1, 2, 3):
                acc = acc + in_q[d, g, zz].astype(F32)
            accs.append(acc)
        acc = jnp.concatenate(accs, axis=0)
        if i > 0:
            mid_q[i] = acc.astype(BF16)
            remote(mid_q.at[i], mid_q_in.at[i], q2_send.at[i], q2_recv.at[i], a, at(zz, xl, y)).start()
        else:
            sum_q = acc
    for i in BACK:
        yy = mod4(y + i)
        accs = []
        for g in range(GROUPS):
            acc = part_o[g, z, yy].astype(F32)
            for d in (1, 2, 3):
                wait(in_o.at[g, d, yy], o1_recv.at[g * 16 + d * 4 + yy])
                acc = acc + in_o[g, d, yy].astype(F32)
            accs.append(acc)
        acc = jnp.concatenate(accs, axis=0)
        if i > 0:
            mid_o[i] = acc.astype(BF16)
            remote(mid_o.at[i], mid_o_in.at[i], o2_send.at[i], o2_recv.at[i], a, at(z, xl, yy)).start()
        else:
            sum_o = acc
    for h in range(2):
        for s in range(2):
            pushed(kvm.at[h], kv_send.at[s * 2 + h], s * 2 + co, at(z, h, y))
            wait(kv.at[0], kr_send.at[s * 2 + h])
    for g in range(GROUPS):
        for h in range(2):
            pushed(mine.at[h, g], s0_send.at[g * 2 + h], z, at(a, h, y))
            for s in range(2):
                n = s * 2 + h
                wait(dkv_mid.at[g, n], dm_send.at[g * 4 + n])
        for k in range(30):
            wait(qa.at[0, g], qa_send.at[g * 30 + k])
        for n in range(16):
            pushed(stat.at[g, n], st_send.at[g * 16 + n], a, at(n // 4, xl, n % 4))
            pushed(norm.at[g], nm_send.at[g * 16 + n], a, at(n // 4, xl, n % 4))
        for d in (1, 2, 3):
            for i in range(4):
                wait(part_o.at[g, 0, 0], o1_send.at[g * 16 + d * 4 + i])
            wait(part_q.at[0, g], q1_send.at[g * 4 + d])
        for n in range(8):
            bias_piece(g, n).wait_send()
    for d in (1, 3, 2):
        wait(mid_q_in.at[d], q2_recv.at[d])
        sum_q = sum_q + mid_q_in[d].astype(F32)
    for d in (1, 3, 2):
        wait(mid_o_in.at[d], o2_recv.at[d])
        sum_o = sum_o + mid_o_in[d].astype(F32)
    for xs in range(2):
        cut = slice(xs * BLK, (xs + 1) * BLK)
        fin_out[xs, 0] = sum_o[:, cut].astype(BF16)
        fin_out[xs, 1] = sum_q[:, cut].astype(BF16)
        push(fin_out.at[xs], fin.at[xl], fin_send.at[xs], fin_recv.at[xl], z, at(a, xs, y))

    hom = jnp.zeros((BLK, WIDTH), F32)
    for g in range(GROUPS):
        for i in range(4):
            wait(dkv_in.at[g, i], dk_recv.at[g * 4 + i])
        for h in range(2):
            acc = (dkv_in[g, h].astype(F32) + dkv_in[g, 2 + h].astype(F32)).astype(BF16)
            cut = slice(h * HALF + g * GW, h * HALF + (g + 1) * GW)
            hom = hom + dot(acc[:, :GW], wk_ref[:, cut], NT) + dot(acc[:, GW:], wv_ref[:, cut], NT)
    for h in range(2):
        wait(fin.at[h], fin_recv.at[h])
        cut = slice(h * HALF, (h + 1) * HALF)
        og = gate[cut, :]
        dl = (gated[cut, :] * fin[h, 0].astype(F32) * og * (1.0 - og)).astype(BF16)
        dq = (fin[h, 1].astype(F32) * SCALE).astype(BF16)
        hom = hom + dot(dq, wq_ref[:, cut], TT) + dot(dl, wg_ref[:, cut], TT)
    hom_ref[...] = hom.astype(BF16)

    for h in range(2):
        pushed(fin_out.at[h], fin_send.at[h], z, at(a, h, y))
        for s in range(2):
            for g in range(GROUPS):
                n = s * 2 + h
                pushed(dkv_sum.at[g, n], dk_send.at[g * 4 + n], s * 2 + co, at(z, h, y))
    for g in range(GROUPS):
        for n in range(8):
            db_own(g, n).wait()
            db_far(g, n).wait()
    for d in (1, 2, 3):
        wait(mid_o.at[d], o2_send.at[d])
        wait(mid_q.at[d], q2_send.at[d])


def on_device(x, g, wq, wk, wv, wg, wr, bias):
    vm = pl.BlockSpec(memory_space=pltpu.VMEM)
    hbm = pl.BlockSpec(memory_space=pl.ANY)
    dma = pltpu.SemaphoreType.DMA
    V = pltpu.VMEM
    hom, db = pl.pallas_call(
        kernel,
        out_shape=[
            jax.ShapeDtypeStruct((BLK, WIDTH), BF16),
            jax.ShapeDtypeStruct((HEADS, ROWS, KEYS), BF16),
        ],
        in_specs=[vm] * 7 + [hbm],
        out_specs=[vm, hbm],
        scratch_shapes=[
            V((2, NH, ROWS, KEYS), BF16),
            V((KEYS, KEYS), BF16),
            V((2, GROUPS, 2, GW, BLK), BF16),
            V((2, 2, HALF, BLK), BF16),
            V((32, GROUPS, 2, GW, BLK), BF16),
            V((8, 2, HALF, KEYS), BF16),
            V((2, SEQS, NH, 2 * KEYS, HD), BF16),
            V((WIDTH, BLK), F32),
            V((WIDTH, BLK), F32),
            V((SEQS, NH, 2 * KEYS, ROWS), F32),
            V((SEQS, NH, 2 * KEYS, ROWS), F32),
            V((GROUPS, 16, 8, CH), F32),
            V((GROUPS, 16, 8, CH), F32),
            V((GROUPS, 8, CH), F32),
            V((GROUPS, 16, 8, CH), F32),
            V((GROUPS, 4, 4, GW, CH), BF16),
            V((4, GROUPS, 4, GW, CH), BF16),
            V((GROUPS, 4, 4, GW, CH), BF16),
            V((4, GROUPS, 4, GW, CH), BF16),
            V((4, HALF, CH), BF16),
            V((4, HALF, CH), BF16),
            V((4, HALF, CH), BF16),
            V((4, HALF, CH), BF16),
            V((2, 2, HALF, BLK), BF16),
            V((2, 2, HALF, BLK), BF16),
            V((SEQS, 2, NH, 2 * KEYS, HD), F32),
            V((GROUPS, 8, KEYS, HALF), BF16),
            V((GROUPS, 4, KEYS, HALF), BF16),
            V((GROUPS, 4, KEYS, HALF), BF16),
            V((GROUPS, 4, KEYS, HALF), BF16),
            V((2, NH, ROWS, KEYS), BF16),
            dma(()), dma((16,)), dma((16,)),
            dma((4,)), dma((60,)), dma((64,)),
            dma((4,)), dma((8,)), dma((4,)),
            dma((32,)), dma((32,)),
            dma((32,)), dma((32,)),
            dma((32,)), dma((32,)),
            dma((8,)), dma((8,)),
            dma((4,)), dma((4,)),
            dma((4,)), dma((4,)),
            dma((2,)), dma((2,)),
            dma((8,)), dma((8,)),
            dma((8,)), dma((8,)),
            dma((16,)), dma((16,)), dma((16,)),
        ],
        compiler_params=pltpu.CompilerParams(
            vmem_limit_bytes=60 * 2 ** 20, has_side_effects=True, collective_id=0),
        cost_estimate=pl.CostEstimate(flops=3 * 10 ** 9, bytes_accessed=10 ** 7, transcendentals=8 * 10 ** 6),
    )(x[0], g[0], wq, wk, wv, wg, wr, bias)
    return hom[None], db.astype(F32)


def solution(mesh):
    return jax.shard_map(
        on_device,
        mesh=mesh,
        in_specs=(
            P("seq", "res", None), P("seq", "res", None), P(), P(), P(), P(), P(),
            P(None, "seq", "res"),
        ),
        out_specs=(P("seq", "res", None), P(None, "seq", "res")),
        check_vma=False,
    )
```
